128 devices in a mesh: row: 8 (over y, core), col: 8 (over x, z_hi), chip: 2 (over z_lo).
Axes of the slice: x: 4, y: 4, z: 4 (z_hi: 2, z_lo: 2; z = z_hi * 2 + z_lo), core: 2. Of those that a mesh axis runs over, the one named last changes fastest.
Arguments:
- pair_input: float32 [512, 512, 128], P('row', ('col', 'chip')), may hold values from -8 to 8
- token_mask: int32 [512], replicated, may hold values from 0 to 1, as said below
- out_stack: bfloat16 [4, 128, 128], P(None, None, 'chip'), may hold values from -0.5 to 0.5
- out_gate: bfloat16 [128, 128], replicated, may hold values from -0.5 to 0.5
- out_final: bfloat16 [128, 128], P('chip'), may hold values from -0.5 to 0.5
- in_stack: bfloat16 [4, 128, 128], P(None, None, 'chip'), may hold values from -0.5 to 0.5
- in_gate: bfloat16 [128, 128], replicated, may hold values from -0.5 to 0.5
- in_final: bfloat16 [128, 128], P('chip'), may hold values from -0.5 to 0.5
- att_stack: bfloat16 [4, 128, 128], P(None, None, 'chip'), may hold values from -3 to 3
- att_bias: bfloat16 [128, 4], P(None, 'chip'), may hold values from -0.5 to 0.5
- att_out: bfloat16 [128, 128], P('chip'), may hold values from -0.5 to 0.5
Outputs:
- pair_output: float32 [512, 512, 128], P('row', ('col', 'chip'))
The draws below stay inside these ranges and needn't reach their ends.
Inputs may be any that keep to these rules, and one draw needn't show every extreme that they name: `token_mask`: 1 on a leading run of tokens and 0 on a nonempty trailing run no longer than 64.
All inputs are finite; a program needn't handle non-finite values.
Results may differ from the reference program's by a relative error of at most 0.029.
Values may be sent and summed in bfloat16 or wider, within the bound.
A program may use at most 128 MiB of HBM per device.

```python
import math
import jax
import jax.numpy as jnp
from jax import lax

C = 128
HID = 128
HEADS = 4
HDIM = 32
TILE = 64
N = 512


def draw_pair_input(key, part):
    key = jax.random.fold_in(key, 11)
    key_scale, key_body = jax.random.split(key, 2)
    channel_scale = jnp.exp(jax.random.uniform(key_scale, (C,), jnp.float32, 0.0, math.log(10.0))) / 5.0
    body_part = jnp.clip(jax.random.normal(key_body, (N, N, C), jnp.float32), -4.0, 4.0)
    return body_part * channel_scale


def draw_token_mask(key, part):
    key = jax.random.fold_in(key, 12)
    dropped = jax.random.randint(key, (), 1, TILE + 1)
    return (jnp.arange(N) < N - dropped).astype(jnp.int32)


def draw_att_stack(key, part):
    key = jax.random.fold_in(key, 13)
    key_base = jax.random.fold_in(key, 0)
    width = HEADS * HDIM
    base_part = jnp.clip(jax.random.normal(key_base, (4, C, width), jnp.float32), -5.0, 5.0) * C ** (-0.5)
    return base_part.astype(jnp.bfloat16)


def levels(stream_key, extent, cuts, smallest, largest):
    def one(position, shards_of):
        heights = jax.random.uniform(jax.random.fold_in(jax.random.fold_in(stream_key, 6), position), (shards_of,), jnp.float32, smallest / len(cuts), largest / len(cuts))
        return jnp.repeat(jnp.exp(heights), extent[position] // shards_of).reshape((-1,) + (1,) * (len(extent) - position - 1))

    factor_of = one(*cuts[0])
    for cut in cuts[1:]:
        factor_of = factor_of * one(*cut)
    return factor_of


def noise(key, dims, deviation, limit, cuts=(), held_as=jnp.bfloat16):
    result = deviation * jax.random.normal(key, dims, jnp.float32)
    if cuts:
        result = result * levels(key, dims, cuts, -0.22, 0.18)
    return jnp.clip(result, -limit, limit).astype(held_as)


def setup_inputs(seed: int = 0) -> dict:
    streams_of = jax.random.split(jax.random.key(seed), 12)
    return {
        "pair_input": draw_pair_input(jax.random.fold_in(streams_of[11], 71), 0),
        "token_mask": draw_token_mask(jax.random.fold_in(streams_of[11], 71), 0),
        "out_stack": noise(streams_of[2], (4, C, HID), C ** -0.5, 0.5, ((2, 2),)),
        "out_gate": noise(streams_of[3], (C, C), C ** -0.5, 0.5),
        "out_final": noise(streams_of[4], (HID, C), HID ** -0.5, 0.5, ((0, 2),)),
        "in_stack": noise(streams_of[5], (4, C, HID), C ** -0.5, 0.5, ((2, 2),)),
        "in_gate": noise(streams_of[6], (C, C), C ** -0.5, 0.5),
        "in_final": noise(streams_of[7], (HID, C), HID ** -0.5, 0.5, ((0, 2),)),
        "att_stack": draw_att_stack(jax.random.fold_in(streams_of[11], 71), 0),
        "att_bias": noise(streams_of[9], (C, HEADS), C ** -0.5, 0.5, ((1, 2),)),
        "att_out": noise(streams_of[10], (HEADS * HDIM, C), (HEADS * HDIM) ** -0.5, 0.5, ((0, 2),)),
    }


epsilon = 1e-05

def layer_norm(values):
    average = lax.optimization_barrier(jnp.mean(values, axis=-1, keepdims=True))
    squares = lax.optimization_barrier(jnp.mean(values * values, axis=-1, keepdims=True))
    return (values - average) * lax.rsqrt(squares - average * average + epsilon)

def project(normed, stack):
    return jnp.einsum('ijc,scd->sijd', normed.astype(jnp.float32), stack.astype(jnp.float32))

def triangle(pair_state, pair_mask, stack, gate_weight, final_weight, outgoing):
    normed = layer_norm(pair_state).astype(jnp.bfloat16)
    projected = project(normed, stack)
    first_arm = (jax.nn.sigmoid(projected[0]) * projected[1] * pair_mask[:, :, None]).astype(jnp.bfloat16)
    second_arm = (jax.nn.sigmoid(projected[2]) * projected[3] * pair_mask[:, :, None]).astype(jnp.bfloat16)
    gating = jax.nn.sigmoid(jnp.einsum('ijc,cd->ijd', normed.astype(jnp.float32), gate_weight.astype(jnp.float32)))
    if outgoing:
        mixture = jnp.einsum('ikd,jkd->ijd', first_arm.astype(jnp.float32), second_arm.astype(jnp.float32))
    else:
        mixture = jnp.einsum('kid,kjd->ijd', first_arm.astype(jnp.float32), second_arm.astype(jnp.float32))
    hidden = layer_norm(mixture).astype(jnp.bfloat16)
    update = jnp.einsum('ijd,dc->ijc', hidden.astype(jnp.float32), final_weight.astype(jnp.float32))
    return pair_state + gating * update

def attend(pair_state, token_mask, stack, bias_weight, out_weight):
    total_tokens = pair_state.shape[0]
    head_count = bias_weight.shape[1]
    normed = layer_norm(pair_state).astype(jnp.bfloat16)
    projected = project(normed, stack)
    head_width = projected.shape[3] // head_count
    queries = projected[0].astype(jnp.bfloat16).reshape(total_tokens, total_tokens, head_count, head_width)
    key_proj = projected[1].astype(jnp.bfloat16).reshape(total_tokens, total_tokens, head_count, head_width)
    values = projected[2].astype(jnp.bfloat16).reshape(total_tokens, total_tokens, head_count, head_width)
    gating = jax.nn.sigmoid(projected[3])
    pair_bias = jnp.einsum('ijc,ch->ijh', normed.astype(jnp.float32), bias_weight.astype(jnp.float32)).astype(jnp.bfloat16)
    bias_keys = jnp.transpose(pair_bias.astype(jnp.float32), (0, 2, 1))
    key_live = token_mask > 0
    inv_root = head_width ** (-0.5)

    def score_block(first_row):
        q_block = lax.dynamic_slice_in_dim(queries, first_row, 8, 0).astype(jnp.float32)
        k_block = lax.dynamic_slice_in_dim(key_proj, first_row, 8, 0).astype(jnp.float32)
        v_block = lax.dynamic_slice_in_dim(values, first_row, 8, 0).astype(jnp.float32)
        scores = jnp.einsum('ijhd,ikhd->ijhk', q_block, k_block) * inv_root + bias_keys[None]
        scores = jnp.where(key_live, scores, -1000000000.0)
        peaks = lax.optimization_barrier(jnp.max(scores, axis=-1, keepdims=True))
        weights = jnp.exp(scores - peaks)
        weights = (weights / lax.optimization_barrier(jnp.sum(weights, axis=-1, keepdims=True))).astype(jnp.bfloat16)
        return jnp.einsum('ijhk,ikhd->ijhd', weights.astype(jnp.float32), v_block)
    block_starts = jnp.arange(total_tokens // 8, dtype=jnp.int32) * 8
    attended = lax.map(score_block, block_starts).reshape(total_tokens, total_tokens, head_count * head_width)
    gated = (gating * attended).astype(jnp.bfloat16)
    return pair_state + jnp.einsum('ijd,dc->ijc', gated.astype(jnp.float32), out_weight.astype(jnp.float32))

def reference(pair_input, token_mask, out_stack, out_gate, out_final, in_stack, in_gate, in_final, att_stack, att_bias, att_out):
    token_float = token_mask.astype(jnp.float32)
    pair_mask = token_float[:, None] * token_float[None, :]
    pair_state = triangle(pair_input, pair_mask, out_stack, out_gate, out_final, True)
    pair_state = triangle(pair_state, pair_mask, in_stack, in_gate, in_final, False)
    return attend(pair_state, token_mask, att_stack, att_bias, att_out)
```

```python
import functools
import math

import jax
import jax.numpy as jnp
from jax import lax
from jax.experimental import pallas as pl
from jax.experimental.pallas import tpu as pltpu
from jax.sharding import PartitionSpec as P

EPS = 1e-05
LOG2E = math.log2(math.e)
MESH = pl.DeviceIdType.MESH
BF = jnp.bfloat16
F32 = jnp.float32
ROWS = 4
GROUPS = 4
TILES = 8
STEP = 45


def dot(a, b, contract):
    return lax.dot_general(a, b, ((contract[:1], contract[1:]), ((), ())), preferred_element_type=F32)


def norm_columns(x):
    mean = jnp.mean(x, axis=0, keepdims=True)
    square = jnp.mean(x * x, axis=0, keepdims=True)
    return (x - mean) * lax.rsqrt(square - mean * mean + EPS)


def kernel(
    sizes,
    x_ref, tm_ref, os_ref, is_ref, as_ref, of_ref, if_ref, ao_ref, ab_ref, og_ref, ig_ref,
    out_ref,
    w_send, wall, w_gate, w_bias, w_fin, mask_o, mask_r,
    xs, xr, state, delta, gate, st_a, st_b, st_c,
    send_out, recv_out, back_out, home_out,
    send_in, recv_in, back_in, home_in,
    arm_a, arm_b,
    normed, bias_st, bias_send, bias_recv, bias_t,
    q_t, k_n, v_t, att, fin_send, fin_recv,
    send_sem, recv_sem,
):
    nr, nc, np_, heads = sizes
    ncp = nc * np_
    n_dev = nr * ncp
    n_ch = n_dev
    half = n_ch // 2
    hdev = n_dev // 2
    n_tok = ROWS * n_dev
    lanes = n_tok // GROUPS
    q_rows = ROWS * GROUPS
    n_pos = ROWS * n_tok
    width = n_pos // TILES
    per = width // lanes
    block_i = n_tok // nr
    block_j = n_tok // ncp
    h_dim = n_ch // heads
    r, c, p = lax.axis_index("row"), lax.axis_index("col"), lax.axis_index("chip")
    cp = c * np_ + p
    me = r * ncp + cp
    core, unit = lax.rem(r, 2), (r // 2) * ncp + cp

    barrier = pltpu.get_barrier_semaphore()

    def place(to):
        return to // ncp, lax.rem(to, ncp) // np_, lax.rem(to, np_)

    def greet(s, carry):
        to = lax.rem(me + s * STEP, n_dev)
        pl.semaphore_signal(barrier, inc=1, device_id=place(to), device_id_type=MESH)
        return carry

    lax.fori_loop(1, n_dev, greet, 0)

    def copy(src, dst, sem, to):
        return pltpu.make_async_remote_copy(
            src_ref=src, dst_ref=dst, send_sem=send_sem.at[sem], recv_sem=recv_sem.at[sem],
            device_id=place(to), device_id_type=MESH,
        )

    def drain(ref, sem):
        pltpu.make_async_copy(ref, ref, sem).wait()

    def span(t, size):
        return pl.ds(pl.multiple_of(t * size, size), size)

    n_first = 4 * half
    base = 3 * n_first
    for t, ref in enumerate((os_ref, is_ref, as_ref)):
        for s in range(4):
            rows = pl.ds((4 * t + s) * half, half)
            w_send[rows, :] = ref[s].astype(F32).T.astype(BF)
    for t, ref in enumerate((of_ref, if_ref, ao_ref)):
        w_send[base + t * half : base + (t + 1) * half, :] = ref[...]
    part = heads // 2
    w_send[base + 3 * half :, :] = jnp.concatenate(
        [ab_ref[...].astype(F32).T, jnp.zeros((16 - part, n_ch), F32)], axis=0
    ).astype(BF)
    wall[pl.ds(p, 1)] = w_send[...][None]
    for t, ref in enumerate((og_ref, ig_ref)):
        w_gate[t] = ref[...].astype(F32).T.astype(BF)

    live = tm_ref[...].astype(F32)
    token = lax.broadcasted_iota(jnp.int32, (lanes, n_tok), 1)
    lane = lax.broadcasted_iota(jnp.int32, (lanes, n_tok), 0)
    live_b = jnp.broadcast_to(live, (lanes, n_tok)).astype(BF)
    pick = (token == r * block_i + lax.rem(lane, block_i)).astype(F32).astype(BF)
    by_i = dot(live_b[:q_rows], pick, (1, 1))
    row_q = lax.broadcasted_iota(jnp.int32, (q_rows, n_tok), 0)
    token_q = lax.broadcasted_iota(jnp.int32, (q_rows, n_tok), 1)
    by_j = [
        dot((token_q == cp * block_j + e * q_rows + row_q).astype(F32).astype(BF), live_b, (1, 1))
        for e in range(2)
    ]
    lane_q = lax.broadcasted_iota(jnp.int32, (q_rows, lanes), 1)
    mask_o[...] = jnp.where(lane_q < block_i, by_j[0], by_j[1]) * by_i
    own = dot((token_q == me * ROWS + row_q // GROUPS).astype(F32).astype(BF), live_b, (1, 1))
    wide_live = jnp.concatenate(
        [live[:, g * lanes : (g + 1) * lanes] for g in range(GROUPS)] * ROWS, axis=0
    )
    mask_r[...] = own * wide_live

    xs[...] = x_ref[...].astype(BF)
    st_a[...] = x_ref[...].reshape(block_i * block_j, n_ch)

    def norm_input(t, carry):
        tile = jnp.concatenate(
            [
                st_a[pl.ds(e * q_rows + t * per + k, block_i, stride=block_j), :]
                for k in range(per)
                for e in range(2)
            ],
            axis=0,
        )
        normed[:, span(t, width)] = norm_columns(tile.T).astype(BF)
        return carry

    lax.fori_loop(0, TILES, norm_input, 0)

    def put_arms(w, h, tile, mask, t):
        proj = dot(w, tile, (1, 0))
        m = half
        first = jax.nn.sigmoid(proj[:m]) * proj[m : 2 * m] * mask
        second = jax.nn.sigmoid(proj[2 * m : 3 * m]) * proj[3 * m :] * mask
        for k in range(per):
            rows = pl.ds(h * (half * q_rows) + t * per + k, half, stride=q_rows)
            st_b[rows, :] = first[:, k * lanes : (k + 1) * lanes]
            st_c[rows, :] = second[:, k * lanes : (k + 1) * lanes]

    def mask_at(ref, t):
        return jnp.concatenate([ref[pl.ds(t * per + k, 1), :] for k in range(per)], axis=1)

    def pack(src, first, count, store):
        n = count // 8

        def body(t, carry):
            at = first + t * n
            rows = pl.ds(pl.multiple_of(at * q_rows, n * q_rows), n * q_rows)
            store(pl.ds(at, n), src[rows, :].reshape(n, q_rows, lanes).astype(BF))
            return carry

        lax.fori_loop(0, 8, body, 0)

    def pack_arms(send, first, count):
        def store_first(at, tile):
            send[at, 0] = tile

        def store_second(at, tile):
            send[at, 1] = tile

        pack(st_b, first, count, store_first)
        pack(st_c, first, count, store_second)

    def out_half(h):
        w = wall[pl.ds(h, 1), :n_first, :].reshape(n_first, n_ch)

        def body(t, carry):
            put_arms(w, h, normed[:, span(t, width)], mask_at(mask_o, t), t)
            return carry

        lax.fori_loop(0, TILES, body, 0)
        pack_arms(send_out, h * half, half)

    def send_half(h):
        def body(s, carry):
            to = h * hdev + lax.rem(me + s * STEP, hdev)
            copy(send_out.at[to], recv_out.at[me], 2, to).start()
            return carry

        lax.fori_loop(1, hdev, body, 0)

        @pl.when(me // hdev != h)
        def _():
            body(0, 0)

    out_half(p)
    pl.semaphore_wait(barrier, n_dev - 1)

    partner = r * ncp + c * np_ + lax.rem(p + 1, np_)
    w_early = copy(w_send.at[pl.ds(0, n_first)], wall.at[p, pl.ds(0, n_first)], 0, partner)
    w_early.start()
    n_late = w_send.shape[0] - n_first
    w_late = copy(w_send.at[pl.ds(n_first, n_late)], wall.at[p, pl.ds(n_first, n_late)], 8, partner)
    w_late.start()
    send_half(p)
    w_early.wait()
    out_half(1 - p)
    send_half(1 - p)

    def send_rows(s, carry):
        to_cp = lax.rem(cp + s, ncp)
        copy(
            xs.at[pl.ds(to_cp * ROWS, ROWS)], xr.at[:, pl.ds(cp * block_j, block_j), :], 1,
            r * ncp + to_cp,
        ).start()
        return carry

    lax.fori_loop(1, ncp, send_rows, 0)
    xr[:, pl.ds(cp * block_j, block_j), :] = xs[pl.ds(cp * ROWS, ROWS)]
    recv_out[pl.ds(me, 1)] = send_out[pl.ds(me, 1)]
    w_late.wait()
    for t in range(3):
        whole = jnp.concatenate(
            [wall[h, base + t * half : base + (t + 1) * half] for h in range(2)], axis=0
        )
        w_fin[t] = whole.astype(F32).T.astype(BF)
    w_bias[...] = jnp.concatenate(
        [wall[h, base + 3 * half : base + 3 * half + 16].astype(F32)[:part] for h in range(2)]
        + [jnp.zeros((8 - heads, n_ch), F32)],
        axis=0,
    ).astype(BF)
    drain(xs.at[pl.ds(0, (ncp - 1) * ROWS)], recv_sem.at[1])

    def load_state(t, carry):
        at = span(t, width)
        row, off = t // (TILES // ROWS), lax.rem(t, TILES // ROWS)
        tile = xr[row, span(off, width), :].astype(F32).T
        state[:, at] = tile
        gate[:, at] = jax.nn.sigmoid(dot(w_gate[0], norm_columns(tile).astype(BF), (1, 0)))
        return carry

    lax.fori_loop(0, TILES, load_state, 0)

    def unpack(load, dst):
        n = n_dev // 8

        def body(t, carry):
            tile = load(t, n).astype(F32).reshape(n * q_rows, lanes)
            dst[span(t, n * q_rows), :] = tile
            return carry

        lax.fori_loop(0, 8, body, 0)

    def all_to_all(src, dst, sem):
        def body(s, carry):
            to = lax.rem(me + s * STEP, n_dev)
            copy(src.at[to], dst.at[me], sem, to).start()
            return carry

        lax.fori_loop(1, n_dev, body, 0)
        dst[pl.ds(me, 1)] = src[pl.ds(me, 1)]

    def arrived(dst, sem):
        drain(dst.at[pl.ds(0, n_dev - 1)], recv_sem.at[sem])

    def update(t, which):
        at = span(t, width)
        hidden = jnp.concatenate(
            [st_a[pl.ds(t * per + k, n_ch, stride=q_rows), :] for k in range(per)], axis=1
        ).astype(BF)
        step = gate[:, at] * dot(w_fin[which], hidden, (1, 0))
        new = state[:, at] + step
        state[:, at] = new
        delta[:, at] = delta[:, at] + step if which else step
        return new

    def mix_and_return(outgoing, back, home, sem):
        n = n_tok // 4
        for m in range(4):
            mixed = dot(arm_a[:, m * n : (m + 1) * n], arm_b[...], (0, 0))
            for g in range(GROUPS):
                rows = pl.ds(m * n * GROUPS + g, n, stride=GROUPS)
                st_a[rows, :] = mixed[:, g * lanes : (g + 1) * lanes]

        def store_back(at, tile):
            back[at] = tile

        pack(st_a, 0, n_dev, store_back)
        all_to_all(back, home, sem)
        arrived(home, sem)
        m = n_dev // 8

        def sums(t, carry):
            tile = home[pl.ds(t * m, m)].astype(F32)
            return carry[0] + jnp.sum(tile, axis=0), carry[1] + jnp.sum(tile * tile, axis=0)

        zero = jnp.zeros((q_rows, lanes), F32)
        total, squares = lax.fori_loop(0, 8, sums, (zero, zero))
        mean = total / n_ch
        scale = lax.rsqrt(squares / n_ch - mean * mean + EPS)

        def normalize(t, carry):
            tile = (home[pl.ds(t * m, m)].astype(F32) - mean[None]) * scale[None]
            st_a[span(t, m * q_rows), :] = tile.reshape(m * q_rows, lanes)
            return carry

        lax.fori_loop(0, 8, normalize, 0)

    arrived(recv_out, 2)
    left = lax.broadcasted_iota(jnp.int32, (ncp * q_rows, lanes), 1) < block_i
    for a, dst in enumerate((arm_a, arm_b)):
        for m in range(nr // 2):
            tiles = [
                recv_out[(2 * m + k) * ncp : (2 * m + k + 1) * ncp, a]
                .astype(F32)
                .reshape(ncp * q_rows, lanes)
                for k in range(2)
            ]
            low = jnp.where(left, tiles[0], pltpu.roll(tiles[1], block_i, 1))
            high = jnp.where(left, pltpu.roll(tiles[0], block_i, 1), tiles[1])
            both = [y.reshape(ncp, 1, q_rows, lanes) for y in (low, high)]
            tile = jnp.concatenate(both, axis=1).reshape(n_tok, lanes)
            dst[:, m * lanes : (m + 1) * lanes] = tile.astype(BF)
    mix_and_return(True, back_out, home_out, 3)

    def project_in(t, carry):
        tile = norm_columns(update(t, 0)).astype(BF)
        mask = mask_at(mask_r, t)
        for h in range(2):
            put_arms(wall[h, n_first : 2 * n_first], h, tile, mask, t)
        gate[:, span(t, width)] = jax.nn.sigmoid(dot(w_gate[1], tile, (1, 0)))
        return carry

    lax.fori_loop(0, TILES, project_in, 0)
    pack_arms(send_in, 0, n_dev)
    all_to_all(send_in, recv_in, 4)
    arrived(recv_in, 4)
    unpack(lambda t, n: recv_in[pl.ds(t * n, n), 0], st_a)
    unpack(lambda t, n: recv_in[pl.ds(t * n, n), 1], st_b)
    for g in range(GROUPS):
        rows = pl.ds(g, n_tok, stride=GROUPS)
        arm_a[:, g * lanes : (g + 1) * lanes] = st_a[rows, :].astype(BF)
        arm_b[:, g * lanes : (g + 1) * lanes] = st_b[rows, :].astype(BF)
    mix_and_return(False, back_in, home_in, 5)

    def bias_step(t, carry):
        tile = norm_columns(update(t, 1)).astype(BF)
        normed[:, span(t, width)] = tile
        proj = dot(w_bias[...], tile, (1, 0)) * LOG2E
        for k in range(per):
            bias_st[pl.ds(t * per + k, 8, stride=q_rows), :] = proj[:, k * lanes : (k + 1) * lanes]
        return carry

    lax.fori_loop(0, TILES, bias_step, 0)
    bias_send[...] = bias_st[: heads * q_rows].astype(BF).reshape(heads, q_rows, lanes)
    for h in range(heads):

        def send_bias(s, carry, h=h):
            other = lax.rem(unit + s * STEP, hdev)
            to = ((other // ncp) * 2 + core) * ncp + lax.rem(other, ncp)
            copy(bias_send.at[h], bias_recv.at[h, core, unit], 10 + h, to).start()
            return carry

        lax.fori_loop(1, hdev, send_bias, 0)
        bias_recv[h, pl.ds(core, 1), pl.ds(unit, 1)] = bias_send[h][None, None]

    def qkvg(t, carry):
        at = span(t, width)
        tile = normed[:, at]
        row, off = t // (TILES // ROWS), lax.rem(t, TILES // ROWS)
        keys = []
        m = half
        for h in range(2):
            proj = dot(wall[h, 2 * n_first : 3 * n_first], tile, (1, 0))
            mine = slice(h * m, (h + 1) * m)
            q_t[mine, at] = (proj[:m] * (LOG2E * h_dim**-0.5)).astype(BF)
            keys.append(proj[m : 2 * m])
            v_t[mine, at] = proj[2 * m : 3 * m].astype(BF)
            gate[mine, at] = jax.nn.sigmoid(proj[3 * m :])
        k_n[row, span(off, width), :] = jnp.concatenate(keys, axis=0).T.astype(BF)
        return carry

    lax.fori_loop(0, TILES, qkvg, 0)
    sibling = (r + 1 - 2 * core) * ncp + cp
    wide = n_tok // 2

    def forward(h):
        drain(bias_recv.at[h, 0, pl.ds(0, hdev - 1)], recv_sem.at[10 + h])
        out = copy(bias_recv.at[h, core], bias_recv.at[h, core], 14 + h, sibling)
        out.start()
        return out

    def finish(i):
        for t in range(TILES // ROWS):
            at = pl.ds(pl.multiple_of(i * n_tok + t * width, width), width)
            gated = (gate[:, at] * att[:, at]).astype(BF)
            total = delta[:, at] + dot(w_fin[2], gated, (1, 0))
            fin_send[i, t * width : (t + 1) * width, :] = total.T.astype(BF)

        def send_final(s, carry):
            to_cp = lax.rem(cp + s, ncp)
            copy(
                fin_send.at[i, pl.ds(to_cp * block_j, block_j), :],
                fin_recv.at[cp * ROWS + i], 7, r * ncp + to_cp,
            ).start()
            return carry

        lax.fori_loop(1, ncp, send_final, 0)

    def attend(h):
        def load(t, n):
            return bias_recv[h, pl.ds(lax.rem(t, 2), 1), pl.ds(t // 2 * n, n)].reshape(n, q_rows, lanes)

        unpack(load, st_a)
        for g in range(GROUPS):
            tile = st_a[pl.ds(g, n_tok, stride=GROUPS), :]
            seen = tm_ref[:, g * lanes : (g + 1) * lanes] > 0
            bias_t[g * lanes : (g + 1) * lanes, :] = jnp.where(seen, tile, -1e30).T
        mine = slice(h * h_dim, (h + 1) * h_dim)

        def body(i, carry):
            keys = k_n[i]
            vals = jnp.concatenate([v_t[mine, span(i, n_tok)], jnp.ones((16, n_tok), BF)], axis=0)
            channel = lax.broadcasted_iota(jnp.int32, (n_ch, wide), 0)
            chosen = (channel >= h * h_dim) & (channel < (h + 1) * h_dim)
            for k in range(2):
                at = pl.ds(pl.multiple_of(i * n_tok + k * wide, wide), wide)
                query = jnp.where(chosen, q_t[:, at].astype(F32), 0.0).astype(BF)
                scores = dot(keys, query, (1, 0)) + bias_t[:, k * wide : (k + 1) * wide]
                peak = jnp.max(scores, axis=0, keepdims=True)
                weights = jnp.exp2(scores - peak).astype(BF)
                got = dot(vals, weights, (1, 0))
                att[mine, at] = got[:h_dim] / got[h_dim : h_dim + 1]
            if h == heads - 1:
                finish(i)
            return carry

        lax.fori_loop(0, ROWS, body, 0)

    forwards = [forward(0)]
    for h in range(heads):
        if h + 1 < heads:
            forwards.append(forward(h + 1))
        forwards[h].wait_recv()
        attend(h)

    fin_recv[pl.ds(cp * ROWS, ROWS)] = fin_send[:, pl.ds(cp * block_j, block_j), :]
    drain(fin_recv.at[pl.ds(0, (ncp - 1) * ROWS)], recv_sem.at[7])
    out_ref[...] = fin_recv[...]

    drain(xs.at[pl.ds(0, (ncp - 1) * ROWS)], send_sem.at[1])
    drain(send_out.at[pl.ds(0, n_dev - 1)], send_sem.at[2])
    drain(back_out.at[pl.ds(0, n_dev - 1)], send_sem.at[3])
    drain(send_in.at[pl.ds(0, n_dev - 1)], send_sem.at[4])
    drain(back_in.at[pl.ds(0, n_dev - 1)], send_sem.at[5])
    drain(fin_recv.at[pl.ds(0, (ncp - 1) * ROWS)], send_sem.at[7])
    for h in range(heads):
        drain(bias_recv.at[h, 0, pl.ds(0, hdev - 1)], send_sem.at[10 + h])
        forwards[h].wait_send()


def on_device(
    sizes, pair_input, token_mask,
    out_stack, out_gate, out_final, in_stack, in_gate, in_final, att_stack, att_bias, att_out,
):
    nr, nc, np_ = sizes
    heads = att_bias.shape[1] * np_
    n_dev = nr * nc * np_
    n_ch = n_dev
    n_tok = ROWS * n_dev
    lanes = n_tok // GROUPS
    q_rows = ROWS * GROUPS
    n_pos = ROWS * n_tok
    vm = pltpu.VMEM
    pair_t = (n_ch, n_pos)
    stage = (n_dev * q_rows, lanes)
    two = (n_dev, 2, q_rows, lanes)
    one = (n_dev, q_rows, lanes)
    w_rows = 15 * (n_ch // 2) + 16
    update = pl.pallas_call(
        functools.partial(kernel, (nr, nc, np_, heads)),
        out_shape=jax.ShapeDtypeStruct(pair_input.shape, BF),
        in_specs=[pl.BlockSpec(memory_space=pltpu.VMEM)] * 11,
        out_specs=pl.BlockSpec(memory_space=pltpu.VMEM),
        scratch_shapes=[
            vm((w_rows, n_ch), BF),
            vm((2, w_rows, n_ch), BF),
            vm((2, n_ch, n_ch), BF),
            vm((8, n_ch), BF),
            vm((3, n_ch, n_ch), BF),
            vm((q_rows, lanes), F32),
            vm((q_rows, lanes), F32),
            vm(pair_input.shape, BF),
            vm((ROWS, n_tok, n_ch), BF),
            vm(pair_t, F32),
            vm(pair_t, F32),
            vm(pair_t, F32),
            vm(stage, F32),
            vm(stage, F32),
            vm(stage, F32),
            vm(two, BF), vm(two, BF), vm(one, BF), vm(one, BF),
            vm(two, BF), vm(two, BF), vm(one, BF), vm(one, BF),
            vm((n_tok, n_tok), BF),
            vm((n_tok, n_tok), BF),
            vm(pair_t, BF),
            vm((8 * q_rows, lanes), F32),
            vm((heads, q_rows, lanes), BF),
            vm((heads, 2, n_dev // 2, q_rows, lanes), BF),
            vm((n_tok, n_tok), F32),
            vm(pair_t, BF),
            vm((ROWS, n_tok, n_ch), BF),
            vm(pair_t, BF),
            vm(pair_t, F32),
            vm((ROWS, n_tok, n_ch), BF),
            vm(pair_input.shape, BF),
            pltpu.SemaphoreType.DMA((18,)),
            pltpu.SemaphoreType.DMA((18,)),
        ],
        compiler_params=pltpu.CompilerParams(
            collective_id=0, has_side_effects=True, vmem_limit_bytes=56 * 2**20
        ),
        name="pair_update",
    )(
        pair_input, token_mask[None, :], out_stack, in_stack, att_stack,
        out_final, in_final, att_out, att_bias, out_gate, in_gate,
    )
    return pair_input + update.astype(F32)


def solution(mesh):
    sizes = tuple(mesh.shape[name] for name in ("row", "col", "chip"))
    return jax.shard_map(
        functools.partial(on_device, sizes),
        mesh=mesh,
        in_specs=(
            P("row", ("col", "chip"), None),
            P(),
            P(None, None, "chip"),
            P(),
            P("chip", None),
            P(None, None, "chip"),
            P(),
            P("chip", None),
            P(None, None, "chip"),
            P(None, "chip"),
            P("chip", None),
        ),
        out_specs=P("row", ("col", "chip"), None),
        check_vma=False,
    )
```

```python
import functools
import math

import jax
import jax.numpy as jnp
from jax import lax
from jax.experimental import pallas as pl
from jax.experimental.pallas import tpu as pltpu
from jax.sharding import PartitionSpec as P

EPS = 1e-05
LOG2E = math.log2(math.e)
MESH = pl.DeviceIdType.MESH
BF = jnp.bfloat16
F32 = jnp.float32
ROWS = 4
GROUPS = 4
TILES = 8
STEP = 45


def dot(a, b, contract):
    return lax.dot_general(a, b, ((contract[:1], contract[1:]), ((), ())), preferred_element_type=F32)


def norm_columns(x):
    mean = jnp.mean(x, axis=0, keepdims=True)
    square = jnp.mean(x * x, axis=0, keepdims=True)
    return (x - mean) * lax.rsqrt(square - mean * mean + EPS)


def kernel(
    sizes,
    x_ref, tm_ref, os_ref, is_ref, as_ref, of_ref, if_ref, ao_ref, ab_ref, og_ref, ig_ref,
    out_ref,
    w_send, wall, w_gate, w_bias, w_fin, mask_o, mask_r,
    xs, xr, state, delta, gate, st_a, st_b, st_c,
    send_out, recv_out, back_out, home_out,
    send_in, recv_in, back_in, home_in,
    arm_a, arm_b,
    normed, bias_st, bias_send, bias_recv, bias_t,
    q_t, k_n, v_t, att, fin_send, fin_recv,
    send_sem, recv_sem,
):
    nr, nc, np_, heads = sizes
    ncp = nc * np_
    n_dev = nr * ncp
    n_ch = n_dev
    half = n_ch // 2
    hdev = n_dev // 2
    n_tok = ROWS * n_dev
    lanes = n_tok // GROUPS
    q_rows = ROWS * GROUPS
    n_pos = ROWS * n_tok
    width = n_pos // TILES
    per = width // lanes
    block_i = n_tok // nr
    block_j = n_tok // ncp
    h_dim = n_ch // heads
    r, c, p = lax.axis_index("row"), lax.axis_index("col"), lax.axis_index("chip")
    cp = c * np_ + p
    me = r * ncp + cp
    core, unit = lax.rem(r, 2), (r // 2) * ncp + cp

    barrier = pltpu.get_barrier_semaphore()

    def place(to):
        return to // ncp, lax.rem(to, ncp) // np_, lax.rem(to, np_)

    for s in range(1, n_dev):
        s = s * STEP % n_dev
        to_r = lax.rem(r + s // ncp, nr)
        to = (to_r, lax.rem(c + s % ncp // np_, nc), lax.rem(p + s % np_, np_))
        pl.semaphore_signal(barrier, inc=1, device_id=to, device_id_type=MESH)

    def copy(src, dst, sem, to):
        return pltpu.make_async_remote_copy(
            src_ref=src, dst_ref=dst, send_sem=send_sem.at[sem], recv_sem=recv_sem.at[sem],
            device_id=place(to), device_id_type=MESH,
        )

    def drain(ref, sem):
        pltpu.make_async_copy(ref, ref, sem).wait()

    def span(t, size):
        return pl.ds(pl.multiple_of(t * size, size), size)

    n_first = 4 * half
    base = 3 * n_first
    for t, ref in enumerate((os_ref, is_ref, as_ref)):
        for s in range(4):
            rows = pl.ds((4 * t + s) * half, half)
            w_send[rows, :] = ref[s]
    for t, ref in enumerate((of_ref, if_ref, ao_ref)):
        w_send[base + t * half : base + (t + 1) * half, :] = ref[...]
    part = heads // 2
    w_send[base + 3 * half :, :] = jnp.concatenate(
        [ab_ref[...].astype(F32), jnp.zeros((16 - part, n_ch), F32)], axis=0
    ).astype(BF)
    wall[pl.ds(p, 1)] = w_send[...][None]
    for t, ref in enumerate((og_ref, ig_ref)):
        w_gate[t] = ref[...].astype(F32).T.astype(BF)

    live = tm_ref[...].astype(F32)
    token = lax.broadcasted_iota(jnp.int32, (lanes, n_tok), 1)
    lane = lax.broadcasted_iota(jnp.int32, (lanes, n_tok), 0)
    live_b = jnp.broadcast_to(live, (lanes, n_tok)).astype(BF)
    pick = (token == r * block_i + lax.rem(lane, block_i)).astype(F32).astype(BF)
    by_i = dot(live_b[:q_rows], pick, (1, 1))
    row_q = lax.broadcasted_iota(jnp.int32, (q_rows, n_tok), 0)
    token_q = lax.broadcasted_iota(jnp.int32, (q_rows, n_tok), 1)
    by_j = [
        dot((token_q == cp * block_j + e * q_rows + row_q).astype(F32).astype(BF), live_b, (1, 1))
        for e in range(2)
    ]
    lane_q = lax.broadcasted_iota(jnp.int32, (q_rows, lanes), 1)
    mask_o[...] = jnp.where(lane_q < block_i, by_j[0], by_j[1]) * by_i
    own = dot((token_q == me * ROWS + row_q // GROUPS).astype(F32).astype(BF), live_b, (1, 1))
    wide_live = jnp.concatenate(
        [live[:, g * lanes : (g + 1) * lanes] for g in range(GROUPS)] * ROWS, axis=0
    )
    mask_r[...] = own * wide_live

    xs[...] = x_ref[...].astype(BF)
    st_a[...] = x_ref[...].reshape(block_i * block_j, n_ch)

    def norm_input(t, carry):
        tile = jnp.concatenate(
            [
                st_a[pl.ds(e * q_rows + t * per + k, block_i, stride=block_j), :]
                for k in range(per)
                for e in range(2)
            ],
            axis=0,
        )
        normed[:, span(t, width)] = norm_columns(tile.T).astype(BF)
        return carry

    lax.fori_loop(0, TILES, norm_input, 0)

    def put_arms(w, h, tile, mask, t):
        proj = dot(w, tile, (1, 0))
        m = half
        first = jax.nn.sigmoid(proj[:m]) * proj[m : 2 * m] * mask
        second = jax.nn.sigmoid(proj[2 * m : 3 * m]) * proj[3 * m :] * mask
        for k in range(per):
            rows = pl.ds(h * (half * q_rows) + t * per + k, half, stride=q_rows)
            st_b[rows, :] = first[:, k * lanes : (k + 1) * lanes]
            st_c[rows, :] = second[:, k * lanes : (k + 1) * lanes]

    def mask_at(ref, t):
        return jnp.concatenate([ref[pl.ds(t * per + k, 1), :] for k in range(per)], axis=1)

    def pack(src, first, count, store):
        n = max(count // 8, 1)

        def body(t, carry):
            at = first + t * n
            rows = pl.ds(pl.multiple_of(at * q_rows, n * q_rows), n * q_rows)
            store(pl.ds(at, n), src[rows, :].reshape(n, q_rows, lanes).astype(BF))
            return carry

        lax.fori_loop(0, count // n, body, 0)

    def pack_arms(send, first, count):
        def store_first(at, tile):
            send[at, 0] = tile

        def store_second(at, tile):
            send[at, 1] = tile

        pack(st_b, first, count, store_first)
        pack(st_c, first, count, store_second)

    def out_half(h):
        w = wall[pl.ds(h, 1), :n_first, :].reshape(n_first, n_ch)

        def body(t, carry):
            put_arms(w, h, normed[:, span(t, width)], mask_at(mask_o, t), t)
            return carry

        lax.fori_loop(0, TILES, body, 0)
        pack_arms(send_out, h * half, half)

    def send_half(h):
        def body(s, carry):
            to = h * hdev + lax.rem(me + s * STEP, hdev)
            copy(send_out.at[to], recv_out.at[me], 2, to).start()
            return carry

        lax.fori_loop(1, hdev, body, 0)

        @pl.when(me // hdev != h)
        def _():
            body(0, 0)

    out_half(p)
    pl.semaphore_wait(barrier, n_dev - 1)

    n_z = 2 * min(nc, 2)
    z = lax.rem(c, 2) * np_ + p if nc > 1 else p
    ways = []
    for step in (1, n_z - 1):
        to_z = lax.rem(z + step, n_z)
        to_c = c // 2 * 2 + to_z // np_ if nc > 1 else c
        ways.append(r * ncp + to_c * np_ + lax.rem(to_z, np_))

    def give(first, count, sem):
        cut = count // 32 * 16
        both = []
        for k, (at, n) in enumerate(((first, cut), (first + cut, count - cut))):
            rows = pl.ds(at, n)
            both.append(copy(w_send.at[rows], wall.at[p, rows], sem + k, ways[k]))
            both[k].start()
        return both

    early = give(0, n_first, 8)
    send_half(p)
    for w_copy in early:
        w_copy.wait()
    out_half(1 - p)
    send_half(1 - p)
    late = give(n_first, w_send.shape[0] - n_first, 18)

    def send_rows(s, carry):
        to_cp = lax.rem(cp + s, ncp)
        copy(
            xs.at[pl.ds(to_cp * ROWS, ROWS)], xr.at[:, pl.ds(cp * block_j, block_j), :], 1,
            r * ncp + to_cp,
        ).start()
        return carry

    lax.fori_loop(1, ncp, send_rows, 0)
    xr[:, pl.ds(cp * block_j, block_j), :] = xs[pl.ds(cp * ROWS, ROWS)]
    recv_out[pl.ds(me, 1)] = send_out[pl.ds(me, 1)]

    def load_rows():
        for w_copy in late:
            w_copy.wait()
        for t in range(3):
            whole = jnp.concatenate(
                [wall[h, base + t * half : base + (t + 1) * half] for h in range(2)], axis=0
            )
            w_fin[t] = whole.astype(F32).T.astype(BF)
        w_bias[...] = jnp.concatenate(
            [wall[h, base + 3 * half : base + 3 * half + 16].astype(F32)[:part] for h in range(2)]
            + [jnp.zeros((8 - heads, n_ch), F32)],
            axis=0,
        ).astype(BF)
        drain(xs.at[pl.ds(0, (ncp - 1) * ROWS)], recv_sem.at[1])

        def load_state(t, carry):
            at = span(t, width)
            row, off = t // (TILES // ROWS), lax.rem(t, TILES // ROWS)
            tile = xr[row, span(off, width), :].astype(F32).T
            state[:, at] = tile
            gate[:, at] = jax.nn.sigmoid(dot(w_gate[0], norm_columns(tile).astype(BF), (1, 0)))
            return carry

        lax.fori_loop(0, TILES, load_state, 0)

    def unpack(load, dst):
        n = n_dev // 8

        def body(t, carry):
            tile = load(t, n).astype(F32).reshape(n * q_rows, lanes)
            dst[span(t, n * q_rows), :] = tile
            return carry

        lax.fori_loop(0, 8, body, 0)

    def arrived(dst, sem):
        drain(dst.at[pl.ds(0, n_dev - 1)], recv_sem.at[sem])

    def update(t, which):
        at = span(t, width)
        hidden = jnp.concatenate(
            [st_a[pl.ds(t * per + k, n_ch, stride=q_rows), :] for k in range(per)], axis=1
        ).astype(BF)
        step = gate[:, at] * dot(w_fin[which], hidden, (1, 0))
        new = state[:, at] + step
        state[:, at] = new
        delta[:, at] = delta[:, at] + step if which else step
        return new

    def mix_and_return(arm_chunk, back, home, sem, meanwhile):
        n = n_tok // 4
        n_to = n_dev // 4
        for k in range(4):
            m = lax.rem(r // 2 + k, 4)
            mixed = dot(arm_chunk(m), arm_b[...], (0, 0))
            for g in range(GROUPS):
                rows = pl.ds(m * (n * GROUPS) + g, n, stride=GROUPS)
                st_c[rows, :] = mixed[:, g * lanes : (g + 1) * lanes]

            def store_back(at, tile):
                back[at] = tile

            pack(st_c, m * n_to, n_to, store_back)

            def body(s, carry, m=m):
                to = m * n_to + lax.rem(me + s * STEP, n_to)
                copy(back.at[to], home.at[me], sem, to).start()
                return carry

            lax.fori_loop(0 if k else 1, n_to, body, 0)
        home[pl.ds(me, 1)] = back[pl.ds(me, 1)]
        meanwhile()
        arrived(home, sem)
        m = n_dev // 8

        def sums(t, carry):
            tile = home[pl.ds(t * m, m)].astype(F32)
            return carry[0] + jnp.sum(tile, axis=0), carry[1] + jnp.sum(tile * tile, axis=0)

        zero = jnp.zeros((q_rows, lanes), F32)
        total, squares = lax.fori_loop(0, 8, sums, (zero, zero))
        mean = total / n_ch
        scale = lax.rsqrt(squares / n_ch - mean * mean + EPS)

        def normalize(t, carry):
            tile = (home[pl.ds(t * m, m)].astype(F32) - mean[None]) * scale[None]
            st_a[span(t, m * q_rows), :] = tile.reshape(m * q_rows, lanes)
            return carry

        lax.fori_loop(0, 8, normalize, 0)

    arrived(recv_out, 2)
    left = lax.broadcasted_iota(jnp.int32, (ncp * q_rows, lanes), 1) < block_i

    def lay_out(m, a):
        tiles = [
            recv_out[pl.ds((2 * m + k) * ncp, ncp), a].astype(F32).reshape(ncp * q_rows, lanes)
            for k in range(2)
        ]
        low = jnp.where(left, tiles[0], pltpu.roll(tiles[1], block_i, 1))
        high = jnp.where(left, pltpu.roll(tiles[0], block_i, 1), tiles[1])
        both = [y.reshape(ncp, 1, q_rows, lanes) for y in (low, high)]
        return jnp.concatenate(both, axis=1).reshape(n_tok, lanes).astype(BF)

    for m in range(4):
        arm_b[:, m * lanes : (m + 1) * lanes] = lay_out(m, 1)
    mix_and_return(lambda m: lay_out(m, 0), back_out, home_out, 3, load_rows)

    own_half = me // hdev

    def in_half(h, first):
        w = wall[pl.ds(h, 1), n_first : 2 * n_first, :].reshape(n_first, n_ch)

        def body(t, carry):
            if first:
                tile = norm_columns(update(t, 0)).astype(BF)
                normed[:, span(t, width)] = tile
            else:
                tile = normed[:, span(t, width)]
            put_arms(w, h, tile, mask_at(mask_r, t), t)
            return carry

        lax.fori_loop(0, TILES, body, 0)
        pack_arms(send_in, h * half, half)

        def send(s, carry):
            to = h * hdev + lax.rem(me + s * STEP, hdev)
            copy(send_in.at[to], recv_in.at[me], 4, to).start()
            return carry

        lax.fori_loop(1 if first else 0, hdev, send, 0)

    in_half(own_half, True)
    in_half(1 - own_half, False)
    recv_in[pl.ds(me, 1)] = send_in[pl.ds(me, 1)]

    def gate_in(t, carry):
        at = span(t, width)
        gate[:, at] = jax.nn.sigmoid(dot(w_gate[1], normed[:, at], (1, 0)))
        return carry

    lax.fori_loop(0, TILES, gate_in, 0)
    arrived(recv_in, 4)
    unpack(lambda t, n: recv_in[pl.ds(t * n, n), 0], st_a)
    unpack(lambda t, n: recv_in[pl.ds(t * n, n), 1], st_b)
    for g in range(GROUPS):
        rows = pl.ds(g, n_tok, stride=GROUPS)
        arm_a[:, g * lanes : (g + 1) * lanes] = st_a[rows, :].astype(BF)
        arm_b[:, g * lanes : (g + 1) * lanes] = st_b[rows, :].astype(BF)
    mix_and_return(lambda m: arm_a[:, span(m, lanes)], back_in, home_in, 5, lambda: None)

    def bias_step(t, carry):
        tile = norm_columns(update(t, 1)).astype(BF)
        normed[:, span(t, width)] = tile
        proj = dot(w_bias[...], tile, (1, 0)) * LOG2E
        for k in range(per):
            bias_st[pl.ds(t * per + k, 8, stride=q_rows), :] = proj[:, k * lanes : (k + 1) * lanes]
        return carry

    lax.fori_loop(0, TILES, bias_step, 0)
    bias_send[...] = bias_st[: heads * q_rows].astype(BF).reshape(heads, q_rows, lanes)
    for h in range(heads):

        def send_bias(s, carry, h=h):
            other = lax.rem(unit + s * STEP, hdev)
            to = ((other // ncp) * 2 + core) * ncp + lax.rem(other, ncp)
            copy(bias_send.at[h], bias_recv.at[h, core, unit], 10 + h, to).start()
            return carry

        lax.fori_loop(1, hdev, send_bias, 0)
        bias_recv[h, pl.ds(core, 1), pl.ds(unit, 1)] = bias_send[h][None, None]

    def qkvg(t, carry):
        at = span(t, width)
        tile = normed[:, at]
        row, off = t // (TILES // ROWS), lax.rem(t, TILES // ROWS)
        keys = []
        m = half
        for h in range(2):
            proj = dot(wall[h, 2 * n_first : 3 * n_first], tile, (1, 0))
            mine = slice(h * m, (h + 1) * m)
            q_t[mine, at] = (proj[:m] * (LOG2E * h_dim**-0.5)).astype(BF)
            keys.append(proj[m : 2 * m])
            v_t[mine, at] = proj[2 * m : 3 * m].astype(BF)
            gate[mine, at] = jax.nn.sigmoid(proj[3 * m :])
        k_n[row, span(off, width), :] = jnp.concatenate(keys, axis=0).T.astype(BF)
        return carry

    lax.fori_loop(0, TILES, qkvg, 0)
    sibling = (r + 1 - 2 * core) * ncp + cp
    wide = n_tok // 2

    def forward(h):
        drain(bias_recv.at[h, 0, pl.ds(0, hdev - 1)], recv_sem.at[10 + h])
        out = copy(bias_recv.at[h, core], bias_recv.at[h, core], 14 + h, sibling)
        out.start()
        return out

    def finish(i):
        for t in range(TILES // ROWS):
            at = pl.ds(pl.multiple_of(i * n_tok + t * width, width), width)
            gated = (gate[:, at] * att[:, at]).astype(BF)
            total = delta[:, at] + dot(w_fin[2], gated, (1, 0))
            fin_send[i, t * width : (t + 1) * width, :] = total.T.astype(BF)

        def send_final(s, carry):
            to_cp = lax.rem(cp + s, ncp)
            copy(
                fin_send.at[i, pl.ds(to_cp * block_j, block_j), :],
                fin_recv.at[cp * ROWS + i], 7, r * ncp + to_cp,
            ).start()
            return carry

        lax.fori_loop(1, ncp, send_final, 0)

    def attend(h):
        def load(t, n):
            return bias_recv[h, pl.ds(lax.rem(t, 2), 1), pl.ds(t // 2 * n, n)].reshape(n, q_rows, lanes)

        unpack(load, st_a)
        for g in range(GROUPS):
            tile = st_a[pl.ds(g, n_tok, stride=GROUPS), :]
            seen = tm_ref[:, g * lanes : (g + 1) * lanes] > 0
            bias_t[g * lanes : (g + 1) * lanes, :] = jnp.where(seen, tile, -1e30).T
        mine = slice(h * h_dim, (h + 1) * h_dim)

        def body(i, carry):
            keys = k_n[i]
            vals = jnp.concatenate([v_t[mine, span(i, n_tok)], jnp.ones((16, n_tok), BF)], axis=0)
            channel = lax.broadcasted_iota(jnp.int32, (n_ch, wide), 0)
            chosen = (channel >= h * h_dim) & (channel < (h + 1) * h_dim)
            for k in range(2):
                at = pl.ds(pl.multiple_of(i * n_tok + k * wide, wide), wide)
                query = jnp.where(chosen, q_t[:, at].astype(F32), 0.0).astype(BF)
                scores = dot(keys, query, (1, 0)) + bias_t[:, k * wide : (k + 1) * wide]
                peak = jnp.max(scores, axis=0, keepdims=True)
                weights = jnp.exp2(scores - peak).astype(BF)
                got = dot(vals, weights, (1, 0))
                att[mine, at] = got[:h_dim] / got[h_dim : h_dim + 1]
            if h == heads - 1:
                finish(i)
            return carry

        lax.fori_loop(0, ROWS, body, 0)

    forwards = [forward(0)]
    for h in range(heads):
        if h + 1 < heads:
            forwards.append(forward(h + 1))
        forwards[h].wait_recv()
        attend(h)

    fin_recv[pl.ds(cp * ROWS, ROWS)] = fin_send[:, pl.ds(cp * block_j, block_j), :]
    drain(fin_recv.at[pl.ds(0, (ncp - 1) * ROWS)], recv_sem.at[7])
    out_ref[...] = fin_recv[...]

    drain(xs.at[pl.ds(0, (ncp - 1) * ROWS)], send_sem.at[1])
    drain(send_out.at[pl.ds(0, n_dev - 1)], send_sem.at[2])
    drain(back_out.at[pl.ds(0, n_dev - 1)], send_sem.at[3])
    drain(send_in.at[pl.ds(0, n_dev - 1)], send_sem.at[4])
    drain(back_in.at[pl.ds(0, n_dev - 1)], send_sem.at[5])
    drain(fin_recv.at[pl.ds(0, (ncp - 1) * ROWS)], send_sem.at[7])
    for h in range(heads):
        drain(bias_recv.at[h, 0, pl.ds(0, hdev - 1)], send_sem.at[10 + h])
        forwards[h].wait_send()


def on_device(
    sizes, pair_input, token_mask,
    out_stack, out_gate, out_final, in_stack, in_gate, in_final, att_stack, att_bias, att_out,
):
    nr, nc, np_ = sizes
    heads = att_bias.shape[1] * np_
    n_dev = nr * nc * np_
    n_ch = n_dev
    n_tok = ROWS * n_dev
    lanes = n_tok // GROUPS
    q_rows = ROWS * GROUPS
    n_pos = ROWS * n_tok
    vm = pltpu.VMEM
    pair_t = (n_ch, n_pos)
    stage = (n_dev * q_rows, lanes)
    two = (n_dev, 2, q_rows, lanes)
    one = (n_dev, q_rows, lanes)
    w_rows = 15 * (n_ch // 2) + 16
    update = pl.pallas_call(
        functools.partial(kernel, (nr, nc, np_, heads)),
        out_shape=jax.ShapeDtypeStruct(pair_input.shape, BF),
        in_specs=[pl.BlockSpec(memory_space=pltpu.VMEM)] * 11,
        out_specs=pl.BlockSpec(memory_space=pltpu.VMEM),
        scratch_shapes=[
            vm((w_rows, n_ch), BF),
            vm((2, w_rows, n_ch), BF),
            vm((2, n_ch, n_ch), BF),
            vm((8, n_ch), BF),
            vm((3, n_ch, n_ch), BF),
            vm((q_rows, lanes), F32),
            vm((q_rows, lanes), F32),
            vm(pair_input.shape, BF),
            vm((ROWS, n_tok, n_ch), BF),
            vm(pair_t, F32),
            vm(pair_t, F32),
            vm(pair_t, F32),
            vm(stage, F32),
            vm(stage, F32),
            vm(stage, F32),
            vm(two, BF), vm(two, BF), vm(one, BF), vm(one, BF),
            vm(two, BF), vm(two, BF), vm(one, BF), vm(one, BF),
            vm((n_tok, n_tok), BF),
            vm((n_tok, n_tok), BF),
            vm(pair_t, BF),
            vm((8 * q_rows, lanes), F32),
            vm((heads, q_rows, lanes), BF),
            vm((heads, 2, n_dev // 2, q_rows, lanes), BF),
            vm((n_tok, n_tok), F32),
            vm(pair_t, BF),
            vm((ROWS, n_tok, n_ch), BF),
            vm(pair_t, BF),
            vm(pair_t, F32),
            vm((ROWS, n_tok, n_ch), BF),
            vm(pair_input.shape, BF),
            pltpu.SemaphoreType.DMA((20,)),
            pltpu.SemaphoreType.DMA((20,)),
        ],
        compiler_params=pltpu.CompilerParams(
            collective_id=0, has_side_effects=True, vmem_limit_bytes=56 * 2**20
        ),
        name="pair_update",
    )(
        pair_input, token_mask[None, :],
        jnp.swapaxes(out_stack, 1, 2), jnp.swapaxes(in_stack, 1, 2), jnp.swapaxes(att_stack, 1, 2),
        out_final, in_final, att_out, att_bias.T, out_gate, in_gate,
    )
    return pair_input + update.astype(F32)


def solution(mesh):
    sizes = tuple(mesh.shape[name] for name in ("row", "col", "chip"))
    return jax.shard_map(
        functools.partial(on_device, sizes),
        mesh=mesh,
        in_specs=(
            P("row", ("col", "chip"), None),
            P(),
            P(None, None, "chip"),
            P(),
            P("chip", None),
            P(None, None, "chip"),
            P(),
            P("chip", None),
            P(None, None, "chip"),
            P(None, "chip"),
            P("chip", None),
        ),
        out_specs=P("row", ("col", "chip"), None),
        check_vma=False,
    )
```

```python
import functools
import math

import jax
import jax.numpy as jnp
from jax import lax
from jax.experimental import pallas as pl
from jax.experimental.pallas import tpu as pltpu
from jax.sharding import PartitionSpec as P

EPS = 1e-05
LOG2E = math.log2(math.e)
MESH = pl.DeviceIdType.MESH
BF = jnp.bfloat16
F32 = jnp.float32
ROWS = 4
GROUPS = 4
TILES = 8
STEP = 45


def dot(a, b, contract):
    return lax.dot_general(a, b, ((contract[:1], contract[1:]), ((), ())), preferred_element_type=F32)


def norm_columns(x):
    mean = jnp.mean(x, axis=0, keepdims=True)
    square = jnp.mean(x * x, axis=0, keepdims=True)
    return (x - mean) * lax.rsqrt(square - mean * mean + EPS)


def kernel(
    sizes,
    x_ref, tm_ref, os_ref, is_ref, as_ref, of_ref, if_ref, ao_ref, ab_ref, og_ref, ig_ref,
    out_ref,
    w_send, wall, w_gate, w_bias, w_fin, mask_o, mask_r,
    xs, xr, state, delta, gate, st_a, st_b, st_c,
    send_out, recv_out, back_out, home_out,
    send_in, recv_in, back_in, home_in,
    arm_a, arm_b,
    normed, bias_st, bias_send, bias_recv, bias_t,
    q_t, k_n, v_t, att, fin_send, fin_recv,
    send_sem, recv_sem,
):
    nr, nc, np_, heads = sizes
    ncp = nc * np_
    n_dev = nr * ncp
    n_ch = n_dev
    half = n_ch // 2
    hdev = n_dev // 2
    n_tok = ROWS * n_dev
    lanes = n_tok // GROUPS
    q_rows = ROWS * GROUPS
    n_pos = ROWS * n_tok
    width = n_pos // TILES
    per = width // lanes
    block_i = n_tok // nr
    block_j = n_tok // ncp
    h_dim = n_ch // heads
    r, c, p = lax.axis_index("row"), lax.axis_index("col"), lax.axis_index("chip")
    cp = c * np_ + p
    me = r * ncp + cp
    core, unit = lax.rem(r, 2), (r // 2) * ncp + cp
    slot = core * hdev + unit

    barrier = pltpu.get_barrier_semaphore()

    def place(to):
        return to // ncp, lax.rem(to, ncp) // np_, lax.rem(to, np_)

    for s in range(1, n_dev):
        s = s * STEP % n_dev
        to_r = lax.rem(r + s // ncp, nr)
        to = (to_r, lax.rem(c + s % ncp // np_, nc), lax.rem(p + s % np_, np_))
        pl.semaphore_signal(barrier, inc=1, device_id=to, device_id_type=MESH)

    def copy(src, dst, sem, to):
        return pltpu.make_async_remote_copy(
            src_ref=src, dst_ref=dst, send_sem=send_sem.at[sem], recv_sem=recv_sem.at[sem],
            device_id=place(to), device_id_type=MESH,
        )

    def drain(ref, sem):
        pltpu.make_async_copy(ref, ref, sem).wait()

    def span(t, size):
        return pl.ds(pl.multiple_of(t * size, size), size)

    n_first = 4 * half
    base = 3 * n_first
    for t, ref in enumerate((os_ref, is_ref, as_ref)):
        for s in range(4):
            rows = pl.ds((4 * t + s) * half, half)
            w_send[rows, :] = ref[s]
    for t, ref in enumerate((of_ref, if_ref, ao_ref)):
        w_send[base + t * half : base + (t + 1) * half, :] = ref[...]
    part = heads // 2
    w_send[base + 3 * half :, :] = jnp.concatenate(
        [ab_ref[...].astype(F32), jnp.zeros((16 - part, n_ch), F32)], axis=0
    ).astype(BF)
    wall[pl.ds(p, 1)] = w_send[...][None]
    for t, ref in enumerate((og_ref, ig_ref)):
        w_gate[t] = ref[...].astype(F32).T.astype(BF)

    live = tm_ref[...].astype(F32)
    token = lax.broadcasted_iota(jnp.int32, (lanes, n_tok), 1)
    lane = lax.broadcasted_iota(jnp.int32, (lanes, n_tok), 0)
    live_b = jnp.broadcast_to(live, (lanes, n_tok)).astype(BF)
    pick = (token == r * block_i + lax.rem(lane, block_i)).astype(F32).astype(BF)
    by_i = dot(live_b[:q_rows], pick, (1, 1))
    row_q = lax.broadcasted_iota(jnp.int32, (q_rows, n_tok), 0)
    token_q = lax.broadcasted_iota(jnp.int32, (q_rows, n_tok), 1)
    by_j = [
        dot((token_q == cp * block_j + e * q_rows + row_q).astype(F32).astype(BF), live_b, (1, 1))
        for e in range(2)
    ]
    lane_q = lax.broadcasted_iota(jnp.int32, (q_rows, lanes), 1)
    mask_o[...] = jnp.where(lane_q < block_i, by_j[0], by_j[1]) * by_i
    own = dot((token_q == me * ROWS + row_q // GROUPS).astype(F32).astype(BF), live_b, (1, 1))
    wide_live = jnp.concatenate(
        [live[:, g * lanes : (g + 1) * lanes] for g in range(GROUPS)] * ROWS, axis=0
    )
    mask_r[...] = own * wide_live

    xs[...] = x_ref[...].astype(BF)
    st_a[...] = x_ref[...].reshape(block_i * block_j, n_ch)

    def norm_input(t, carry):
        tile = jnp.concatenate(
            [
                st_a[pl.ds(e * q_rows + t * per + k, block_i, stride=block_j), :]
                for k in range(per)
                for e in range(2)
            ],
            axis=0,
        )
        normed[:, span(t, width)] = norm_columns(tile.T).astype(BF)
        return carry

    lax.fori_loop(0, TILES, norm_input, 0)

    def put_arms(w, h, tile, mask, t):
        proj = dot(w, tile, (1, 0))
        m = half
        first = jax.nn.sigmoid(proj[:m]) * proj[m : 2 * m] * mask
        second = jax.nn.sigmoid(proj[2 * m : 3 * m]) * proj[3 * m :] * mask
        for k in range(per):
            rows = pl.ds(h * (half * q_rows) + t * per + k, half, stride=q_rows)
            st_b[rows, :] = first[:, k * lanes : (k + 1) * lanes]
            st_c[rows, :] = second[:, k * lanes : (k + 1) * lanes]

    def mask_at(ref, t):
        return jnp.concatenate([ref[pl.ds(t * per + k, 1), :] for k in range(per)], axis=1)

    def pack(src, first, count, store):
        n = max(count // 8, 1)

        def body(t, carry):
            at = first + t * n
            rows = pl.ds(pl.multiple_of(at * q_rows, n * q_rows), n * q_rows)
            store(pl.ds(at, n), src[rows, :].reshape(n, q_rows, lanes).astype(BF))
            return carry

        lax.fori_loop(0, count // n, body, 0)

    def pack_arms(send, first, count):
        def store_first(at, tile):
            send[at, 0] = tile

        def store_second(at, tile):
            send[at, 1] = tile

        pack(st_b, first, count, store_first)
        pack(st_c, first, count, store_second)

    def out_half(h):
        w = wall[pl.ds(h, 1), :n_first, :].reshape(n_first, n_ch)

        def body(t, carry):
            put_arms(w, h, normed[:, span(t, width)], mask_at(mask_o, t), t)
            return carry

        lax.fori_loop(0, TILES, body, 0)
        pack_arms(send_out, h * half, half)

    def send_half(send, recv, sem, h):
        def body(s, carry):
            other = lax.rem(unit + s * STEP, hdev)
            to = ((other // ncp) * 2 + h) * ncp + lax.rem(other, ncp)
            copy(send.at[h * hdev + other], recv.at[me], sem, to).start()
            return carry

        lax.fori_loop(1, hdev, body, 0)

        @pl.when(core != h)
        def _():
            body(0, 0)

    out_half(p)
    pl.semaphore_wait(barrier, n_dev - 1)

    n_z = 2 * min(nc, 2)
    z = lax.rem(c, 2) * np_ + p if nc > 1 else p
    ways = []
    for step in (1, n_z - 1):
        to_z = lax.rem(z + step, n_z)
        to_c = c // 2 * 2 + to_z // np_ if nc > 1 else c
        ways.append(r * ncp + to_c * np_ + lax.rem(to_z, np_))

    def give(first, count, sem):
        cut = count // 32 * 16
        both = []
        for k, (at, n) in enumerate(((first, cut), (first + cut, count - cut))):
            rows = pl.ds(at, n)
            both.append(copy(w_send.at[rows], wall.at[p, rows], sem + k, ways[k]))
            both[k].start()
        return both

    early = give(0, n_first, 8)
    send_half(send_out, recv_out, 2, p)
    for w_copy in early:
        w_copy.wait()
    out_half(1 - p)
    send_half(send_out, recv_out, 2, 1 - p)
    late = give(n_first, w_send.shape[0] - n_first, 18)

    def send_rows(s, carry):
        to_cp = lax.rem(cp + s, ncp)
        copy(
            xs.at[pl.ds(to_cp * ROWS, ROWS)], xr.at[:, pl.ds(cp * block_j, block_j), :], 1,
            r * ncp + to_cp,
        ).start()
        return carry

    lax.fori_loop(1, ncp, send_rows, 0)
    xr[:, pl.ds(cp * block_j, block_j), :] = xs[pl.ds(cp * ROWS, ROWS)]
    recv_out[pl.ds(me, 1)] = send_out[pl.ds(slot, 1)]

    def load_rows():
        for w_copy in late:
            w_copy.wait()
        for t in range(3):
            whole = jnp.concatenate(
                [wall[h, base + t * half : base + (t + 1) * half] for h in range(2)], axis=0
            )
            w_fin[t] = whole.astype(F32).T.astype(BF)
        w_bias[...] = jnp.concatenate(
            [wall[h, base + 3 * half : base + 3 * half + 16].astype(F32)[:part] for h in range(2)]
            + [jnp.zeros((8 - heads, n_ch), F32)],
            axis=0,
        ).astype(BF)
        drain(xs.at[pl.ds(0, (ncp - 1) * ROWS)], recv_sem.at[1])

        def load_state(t, carry):
            at = span(t, width)
            row, off = t // (TILES // ROWS), lax.rem(t, TILES // ROWS)
            tile = xr[row, span(off, width), :].astype(F32).T
            state[:, at] = tile
            gate[:, at] = jax.nn.sigmoid(dot(w_gate[0], norm_columns(tile).astype(BF), (1, 0)))
            return carry

        lax.fori_loop(0, TILES, load_state, 0)

    def unpack(load, dst):
        n = n_dev // 8

        def body(t, carry):
            tile = load(t, n).astype(F32).reshape(n * q_rows, lanes)
            dst[span(t, n * q_rows), :] = tile
            return carry

        lax.fori_loop(0, 8, body, 0)

    def arrived(dst, sem):
        drain(dst.at[pl.ds(0, n_dev - 1)], recv_sem.at[sem])

    def update(t, which):
        at = span(t, width)
        hidden = jnp.concatenate(
            [st_a[pl.ds(t * per + k, n_ch, stride=q_rows), :] for k in range(per)], axis=1
        ).astype(BF)
        step = gate[:, at] * dot(w_fin[which], hidden, (1, 0))
        new = state[:, at] + step
        state[:, at] = new
        delta[:, at] = delta[:, at] + step if which else step
        return new

    def mix_and_return(arm_chunk, back, home, sem, meanwhile):
        n = n_tok // 4
        n_to = n_dev // 4
        y, x, z_of = r // 2, c // np_, lax.rem(c, 2) * np_ + p
        for k in range(4):
            ahead = lax.rem(k + x + z_of, 4)
            m = lax.rem(jnp.where(lax.rem(y, 2) == 0, y + ahead, y + 4 - ahead), 4)
            mixed = dot(arm_chunk(m), arm_b[...], (0, 0))
            for g in range(GROUPS):
                rows = pl.ds(m * (n * GROUPS) + g, n, stride=GROUPS)
                st_c[rows, :] = mixed[:, g * lanes : (g + 1) * lanes]

            def store_back(at, tile):
                back[at] = tile

            pack(st_c, m * n_to, n_to, store_back)

            def body(s, carry, m=m):
                to = m * n_to + lax.rem(me + s * STEP, n_to)
                copy(back.at[to], home.at[slot], sem, to).start()
                return carry

            lax.fori_loop(1, n_to, body, 0)

            @pl.when(m != y)
            def _(body=body):
                body(0, 0)

        home[pl.ds(slot, 1)] = back[pl.ds(me, 1)]
        meanwhile()
        arrived(home, sem)
        m = n_dev // 8

        def sums(t, carry):
            tile = home[pl.ds(t * m, m)].astype(F32)
            return carry[0] + jnp.sum(tile, axis=0), carry[1] + jnp.sum(tile * tile, axis=0)

        zero = jnp.zeros((q_rows, lanes), F32)
        total, squares = lax.fori_loop(0, 8, sums, (zero, zero))
        mean = total / n_ch
        scale = lax.rsqrt(squares / n_ch - mean * mean + EPS)

        def normalize(t, carry):
            tile = (home[pl.ds(t * m, m)].astype(F32) - mean[None]) * scale[None]
            st_a[span(t, m * q_rows), :] = tile.reshape(m * q_rows, lanes)
            return carry

        lax.fori_loop(0, 8, normalize, 0)

    arrived(recv_out, 2)
    left = lax.broadcasted_iota(jnp.int32, (ncp * q_rows, lanes), 1) < block_i

    def lay_out(m, a):
        tiles = [
            recv_out[pl.ds((2 * m + k) * ncp, ncp), a].astype(F32).reshape(ncp * q_rows, lanes)
            for k in range(2)
        ]
        low = jnp.where(left, tiles[0], pltpu.roll(tiles[1], block_i, 1))
        high = jnp.where(left, pltpu.roll(tiles[0], block_i, 1), tiles[1])
        both = [y.reshape(ncp, 1, q_rows, lanes) for y in (low, high)]
        return jnp.concatenate(both, axis=1).reshape(n_tok, lanes).astype(BF)

    for m in range(4):
        arm_b[:, m * lanes : (m + 1) * lanes] = lay_out(m, 1)
    mix_and_return(lambda m: lay_out(m, 0), back_out, home_out, 3, load_rows)

    def in_half(h, first):
        w = wall[pl.ds(h, 1), n_first : 2 * n_first, :].reshape(n_first, n_ch)

        def body(t, carry):
            if first:
                tile = norm_columns(update(t, 0)).astype(BF)
                normed[:, span(t, width)] = tile
            else:
                tile = normed[:, span(t, width)]
            put_arms(w, h, tile, mask_at(mask_r, t), t)
            return carry

        lax.fori_loop(0, TILES, body, 0)
        pack_arms(send_in, h * half, half)
        send_half(send_in, recv_in, 4, h)

    in_half(0, True)
    in_half(1, False)
    recv_in[pl.ds(me, 1)] = send_in[pl.ds(slot, 1)]

    def gate_in(t, carry):
        at = span(t, width)
        gate[:, at] = jax.nn.sigmoid(dot(w_gate[1], normed[:, at], (1, 0)))
        return carry

    lax.fori_loop(0, TILES, gate_in, 0)
    arrived(recv_in, 4)
    unpack(lambda t, n: recv_in[pl.ds(t * n, n), 0], st_a)
    unpack(lambda t, n: recv_in[pl.ds(t * n, n), 1], st_b)
    for g in range(GROUPS):
        rows = pl.ds(g, n_tok, stride=GROUPS)
        arm_a[:, g * lanes : (g + 1) * lanes] = st_a[rows, :].astype(BF)
        arm_b[:, g * lanes : (g + 1) * lanes] = st_b[rows, :].astype(BF)
    mix_and_return(lambda m: arm_a[:, span(m, lanes)], back_in, home_in, 5, lambda: None)

    def bias_step(t, carry):
        tile = norm_columns(update(t, 1)).astype(BF)
        normed[:, span(t, width)] = tile
        proj = dot(w_bias[...], tile, (1, 0)) * LOG2E
        for k in range(per):
            bias_st[pl.ds(t * per + k, 8, stride=q_rows), :] = proj[:, k * lanes : (k + 1) * lanes]
        return carry

    lax.fori_loop(0, TILES, bias_step, 0)
    bias_send[...] = bias_st[: heads * q_rows].astype(BF).reshape(heads, q_rows, lanes)
    for h in range(heads):

        def send_bias(s, carry, h=h):
            other = lax.rem(unit + s * STEP, hdev)
            to = ((other // ncp) * 2 + core) * ncp + lax.rem(other, ncp)
            copy(bias_send.at[h], bias_recv.at[h, core, unit], 10 + h, to).start()
            return carry

        lax.fori_loop(1, hdev, send_bias, 0)
        bias_recv[h, pl.ds(core, 1), pl.ds(unit, 1)] = bias_send[h][None, None]

    def qkvg(t, carry):
        at = span(t, width)
        tile = normed[:, at]
        row, off = t // (TILES // ROWS), lax.rem(t, TILES // ROWS)
        keys = []
        m = half
        for h in range(2):
            proj = dot(wall[h, 2 * n_first : 3 * n_first], tile, (1, 0))
            mine = slice(h * m, (h + 1) * m)
            q_t[mine, at] = (proj[:m] * (LOG2E * h_dim**-0.5)).astype(BF)
            keys.append(proj[m : 2 * m])
            v_t[mine, at] = proj[2 * m : 3 * m].astype(BF)
            gate[mine, at] = jax.nn.sigmoid(proj[3 * m :])
        k_n[row, span(off, width), :] = jnp.concatenate(keys, axis=0).T.astype(BF)
        return carry

    lax.fori_loop(0, TILES, qkvg, 0)
    sibling = (r + 1 - 2 * core) * ncp + cp
    def forward(h):
        drain(bias_recv.at[h, 0, pl.ds(0, hdev - 1)], recv_sem.at[10 + h])
        out = copy(bias_recv.at[h, core], bias_recv.at[h, core], 14 + h, sibling)
        out.start()
        return out

    def finish(i):
        for t in range(TILES // ROWS):
            at = slice(i * n_tok + t * width, i * n_tok + (t + 1) * width)
            gated = (gate[:, at] * att[:, at]).astype(BF)
            total = delta[:, at] + dot(w_fin[2], gated, (1, 0))
            fin_send[i, t * width : (t + 1) * width, :] = total.T.astype(BF)

        def send_final(s, carry):
            to_cp = lax.rem(cp + s, ncp)
            copy(
                fin_send.at[i, pl.ds(to_cp * block_j, block_j), :],
                fin_recv.at[cp * ROWS + i], 7, r * ncp + to_cp,
            ).start()
            return carry

        lax.fori_loop(1, ncp, send_final, 0)

    def attend(h):
        def load(t, n):
            return bias_recv[h, pl.ds(lax.rem(t, 2), 1), pl.ds(t // 2 * n, n)].reshape(n, q_rows, lanes)

        unpack(load, st_a)
        for g in range(GROUPS):
            tile = st_a[pl.ds(g, n_tok, stride=GROUPS), :]
            seen = tm_ref[:, g * lanes : (g + 1) * lanes] > 0
            bias_t[g * lanes : (g + 1) * lanes, :] = jnp.where(seen, tile, -1e30).T
        mine = slice(h * h_dim, (h + 1) * h_dim)

        channel = lax.broadcasted_iota(jnp.int32, (n_ch, n_tok), 0)
        chosen = (channel >= h * h_dim) & (channel < (h + 1) * h_dim)

        def scores_of(i):
            query = q_t[:, i * n_tok : (i + 1) * n_tok].astype(F32)
            return dot(k_n[i], jnp.where(chosen, query, 0.0).astype(BF), (1, 0)) + bias_t[...]

        following = scores_of(0)
        for i in range(ROWS):
            scores = following
            if i + 1 < ROWS:
                following = scores_of(i + 1)
            at = slice(i * n_tok, (i + 1) * n_tok)
            vals = jnp.concatenate([v_t[mine, at], jnp.ones((16, n_tok), BF)], axis=0)
            peak = jnp.max(scores, axis=0, keepdims=True)
            got = dot(vals, jnp.exp2(scores - peak).astype(BF), (1, 0))
            att[mine, at] = got[:h_dim] / got[h_dim : h_dim + 1]
            if h == heads - 1:
                finish(i)

    forwards = [forward(0)]
    for h in range(heads):
        if h + 1 < heads:
            forwards.append(forward(h + 1))
        forwards[h].wait_recv()
        attend(h)

    fin_recv[pl.ds(cp * ROWS, ROWS)] = fin_send[:, pl.ds(cp * block_j, block_j), :]
    drain(fin_recv.at[pl.ds(0, (ncp - 1) * ROWS)], recv_sem.at[7])
    out_ref[...] = fin_recv[...]

    drain(xs.at[pl.ds(0, (ncp - 1) * ROWS)], send_sem.at[1])
    drain(send_out.at[pl.ds(0, n_dev - 1)], send_sem.at[2])
    drain(back_out.at[pl.ds(0, n_dev - 1)], send_sem.at[3])
    drain(send_in.at[pl.ds(0, n_dev - 1)], send_sem.at[4])
    drain(back_in.at[pl.ds(0, n_dev - 1)], send_sem.at[5])
    drain(fin_recv.at[pl.ds(0, (ncp - 1) * ROWS)], send_sem.at[7])
    for h in range(heads):
        drain(bias_recv.at[h, 0, pl.ds(0, hdev - 1)], send_sem.at[10 + h])
        forwards[h].wait_send()


def on_device(
    sizes, pair_input, token_mask,
    out_stack, out_gate, out_final, in_stack, in_gate, in_final, att_stack, att_bias, att_out,
):
    nr, nc, np_ = sizes
    heads = att_bias.shape[1] * np_
    n_dev = nr * nc * np_
    n_ch = n_dev
    n_tok = ROWS * n_dev
    lanes = n_tok // GROUPS
    q_rows = ROWS * GROUPS
    n_pos = ROWS * n_tok
    vm = pltpu.VMEM
    pair_t = (n_ch, n_pos)
    stage = (n_dev * q_rows, lanes)
    two = (n_dev, 2, q_rows, lanes)
    one = (n_dev, q_rows, lanes)
    w_rows = 15 * (n_ch // 2) + 16
    update = pl.pallas_call(
        functools.partial(kernel, (nr, nc, np_, heads)),
        out_shape=jax.ShapeDtypeStruct(pair_input.shape, BF),
        in_specs=[pl.BlockSpec(memory_space=pltpu.VMEM)] * 11,
        out_specs=pl.BlockSpec(memory_space=pltpu.VMEM),
        scratch_shapes=[
            vm((w_rows, n_ch), BF),
            vm((2, w_rows, n_ch), BF),
            vm((2, n_ch, n_ch), BF),
            vm((8, n_ch), BF),
            vm((3, n_ch, n_ch), BF),
            vm((q_rows, lanes), F32),
            vm((q_rows, lanes), F32),
            vm(pair_input.shape, BF),
            vm((ROWS, n_tok, n_ch), BF),
            vm(pair_t, F32),
            vm(pair_t, F32),
            vm(pair_t, F32),
            vm(stage, F32),
            vm(stage, F32),
            vm(stage, F32),
            vm(two, BF), vm(two, BF), vm(one, BF), vm(one, BF),
            vm(two, BF), vm(two, BF), vm(one, BF), vm(one, BF),
            vm((n_tok, n_tok), BF),
            vm((n_tok, n_tok), BF),
            vm(pair_t, BF),
            vm((8 * q_rows, lanes), F32),
            vm((heads, q_rows, lanes), BF),
            vm((heads, 2, n_dev // 2, q_rows, lanes), BF),
            vm((n_tok, n_tok), F32),
            vm(pair_t, BF),
            vm((ROWS, n_tok, n_ch), BF),
            vm(pair_t, BF),
            vm(pair_t, F32),
            vm((ROWS, n_tok, n_ch), BF),
            vm(pair_input.shape, BF),
            pltpu.SemaphoreType.DMA((20,)),
            pltpu.SemaphoreType.DMA((20,)),
        ],
        compiler_params=pltpu.CompilerParams(
            collective_id=0, has_side_effects=True, vmem_limit_bytes=56 * 2**20
        ),
        name="pair_update",
    )(
        pair_input, token_mask[None, :],
        jnp.swapaxes(out_stack, 1, 2), jnp.swapaxes(in_stack, 1, 2), jnp.swapaxes(att_stack, 1, 2),
        out_final, in_final, att_out, att_bias.T, out_gate, in_gate,
    )
    return pair_input + update.astype(F32)


def solution(mesh):
    sizes = tuple(mesh.shape[name] for name in ("row", "col", "chip"))
    return jax.shard_map(
        functools.partial(on_device, sizes),
        mesh=mesh,
        in_specs=(
            P("row", ("col", "chip"), None),
            P(),
            P(None, None, "chip"),
            P(),
            P("chip", None),
            P(None, None, "chip"),
            P(),
            P("chip", None),
            P(None, None, "chip"),
            P(None, "chip"),
            P("chip", None),
        ),
        out_specs=P("row", ("col", "chip"), None),
        check_vma=False,
    )
```

```python
import functools
import math

import jax
import jax.numpy as jnp
from jax import lax
from jax.experimental import pallas as pl
from jax.experimental.pallas import tpu as pltpu
from jax.sharding import PartitionSpec as P

EPS = 1e-05
LOG2E = math.log2(math.e)
MESH = pl.DeviceIdType.MESH
BF = jnp.bfloat16
F32 = jnp.float32
ROWS = 4
GROUPS = 4
TILES = 8
STEP = 45


def dot(a, b, contract):
    return lax.dot_general(a, b, ((contract[:1], contract[1:]), ((), ())), preferred_element_type=F32)


def steps(count, body):
    for t in range(count):
        body(t)


def norm_columns(x):
    mean = jnp.mean(x, axis=0, keepdims=True)
    square = jnp.mean(x * x, axis=0, keepdims=True)
    return (x - mean) * lax.rsqrt(square - mean * mean + EPS)


def kernel(
    sizes,
    x_ref, tm_ref, os_ref, is_ref, as_ref, of_ref, if_ref, ao_ref, ab_ref, og_ref, ig_ref,
    out_ref,
    w_send, wall, w_gate, w_bias, w_fin, mask_o, mask_r,
    xs, xr, state, delta, gate, st_a, st_b, st_c,
    send_out, recv_out, back_out, home_out,
    send_in, recv_in, back_in, home_in,
    arm_a, arm_b,
    normed, bias_st, bias_send, bias_recv, bias_t,
    q_t, k_n, v_t, att, fin_send, fin_recv,
    send_sem, recv_sem,
):
    nr, nc, np_, heads = sizes
    ncp = nc * np_
    n_dev = nr * ncp
    n_ch = n_dev
    half = n_ch // 2
    hdev = n_dev // 2
    n_tok = ROWS * n_dev
    lanes = n_tok // GROUPS
    q_rows = ROWS * GROUPS
    n_pos = ROWS * n_tok
    width = n_pos // TILES
    per = width // lanes
    block_i = n_tok // nr
    block_j = n_tok // ncp
    h_dim = n_ch // heads
    r, c, p = lax.axis_index("row"), lax.axis_index("col"), lax.axis_index("chip")
    cp = c * np_ + p
    me = r * ncp + cp
    core, unit = lax.rem(r, 2), (r // 2) * ncp + cp
    slot = core * hdev + unit

    barrier = pltpu.get_barrier_semaphore()

    def place(to):
        return to // ncp, lax.rem(to, ncp) // np_, lax.rem(to, np_)

    for s in range(1, n_dev):
        s = s * STEP % n_dev
        to_r = lax.rem(r + s // ncp, nr)
        to = (to_r, lax.rem(c + s % ncp // np_, nc), lax.rem(p + s % np_, np_))
        pl.semaphore_signal(barrier, inc=1, device_id=to, device_id_type=MESH)

    def copy(src, dst, sem, to):
        return pltpu.make_async_remote_copy(
            src_ref=src, dst_ref=dst, send_sem=send_sem.at[sem], recv_sem=recv_sem.at[sem],
            device_id=place(to), device_id_type=MESH,
        )

    def drain(ref, sem):
        pltpu.make_async_copy(ref, ref, sem).wait()

    def span(t, size):
        at = t * size
        return pl.ds(at if isinstance(at, int) else pl.multiple_of(at, size), size)

    n_first = 4 * half
    base = 3 * n_first
    for t, ref in enumerate((os_ref, is_ref, as_ref)):
        for s in range(4):
            rows = pl.ds((4 * t + s) * half, half)
            w_send[rows, :] = ref[s]
    for t, ref in enumerate((of_ref, if_ref, ao_ref)):
        w_send[base + t * half : base + (t + 1) * half, :] = ref[...]
    part = heads // 2
    w_send[base + 3 * half :, :] = jnp.concatenate(
        [ab_ref[...].astype(F32), jnp.zeros((16 - part, n_ch), F32)], axis=0
    ).astype(BF)
    wall[pl.ds(p, 1)] = w_send[...][None]
    for t, ref in enumerate((og_ref, ig_ref)):
        w_gate[t] = ref[...].astype(F32).T.astype(BF)

    live = tm_ref[...].astype(F32)
    token = lax.broadcasted_iota(jnp.int32, (lanes, n_tok), 1)
    lane = lax.broadcasted_iota(jnp.int32, (lanes, n_tok), 0)
    live_b = jnp.broadcast_to(live, (lanes, n_tok)).astype(BF)
    pick = (token == r * block_i + lax.rem(lane, block_i)).astype(F32).astype(BF)
    by_i = dot(live_b[:q_rows], pick, (1, 1))
    row_q = lax.broadcasted_iota(jnp.int32, (q_rows, n_tok), 0)
    token_q = lax.broadcasted_iota(jnp.int32, (q_rows, n_tok), 1)
    by_j = [
        dot((token_q == cp * block_j + e * q_rows + row_q).astype(F32).astype(BF), live_b, (1, 1))
        for e in range(2)
    ]
    lane_q = lax.broadcasted_iota(jnp.int32, (q_rows, lanes), 1)
    mask_o[...] = jnp.where(lane_q < block_i, by_j[0], by_j[1]) * by_i
    own = dot((token_q == me * ROWS + row_q // GROUPS).astype(F32).astype(BF), live_b, (1, 1))
    wide_live = jnp.concatenate(
        [live[:, g * lanes : (g + 1) * lanes] for g in range(GROUPS)] * ROWS, axis=0
    )
    mask_r[...] = own * wide_live

    xs[...] = x_ref[...].astype(BF)
    st_a[...] = x_ref[...].reshape(block_i * block_j, n_ch)

    def norm_input(t):
        tile = jnp.concatenate(
            [
                st_a[pl.ds(e * q_rows + t * per + k, block_i, stride=block_j), :]
                for k in range(per)
                for e in range(2)
            ],
            axis=0,
        )
        normed[:, span(t, width)] = norm_columns(tile.T).astype(BF)

    steps(TILES, norm_input)

    def put_arms(w, h, tile, mask, t):
        proj = dot(w, tile, (1, 0))
        m = half
        first = jax.nn.sigmoid(proj[:m]) * proj[m : 2 * m] * mask
        second = jax.nn.sigmoid(proj[2 * m : 3 * m]) * proj[3 * m :] * mask
        for k in range(per):
            rows = pl.ds(h * (half * q_rows) + t * per + k, half, stride=q_rows)
            st_b[rows, :] = first[:, k * lanes : (k + 1) * lanes]
            st_c[rows, :] = second[:, k * lanes : (k + 1) * lanes]

    def mask_at(ref, t):
        return jnp.concatenate([ref[pl.ds(t * per + k, 1), :] for k in range(per)], axis=1)

    def pack(src, first, count, store):
        n = max(count // 8, 1)

        def body(t):
            at = first + t * n
            start = at * q_rows
            if not isinstance(at, int):
                start = pl.multiple_of(start, n * q_rows)
            rows = pl.ds(start, n * q_rows)
            store(pl.ds(at, n), src[rows, :].reshape(n, q_rows, lanes).astype(BF))

        steps(count // n, body)

    def pack_arms(send, first, count):
        def store_first(at, tile):
            send[at, 0] = tile

        def store_second(at, tile):
            send[at, 1] = tile

        pack(st_b, first, count, store_first)
        pack(st_c, first, count, store_second)

    def out_half(h):
        w = wall[pl.ds(h, 1), :n_first, :].reshape(n_first, n_ch)

        def body(t):
            put_arms(w, h, normed[:, span(t, width)], mask_at(mask_o, t), t)

        steps(TILES, body)
        pack_arms(send_out, h * half, half)

    def send_half(send, recv, sem, h):
        def body(s, carry):
            other = lax.rem(unit + s * STEP, hdev)
            to = ((other // ncp) * 2 + h) * ncp + lax.rem(other, ncp)
            copy(send.at[h * hdev + other], recv.at[me], sem, to).start()
            return carry

        lax.fori_loop(1, hdev, body, 0)

        @pl.when(core != h)
        def _():
            body(0, 0)

    out_half(p)
    pl.semaphore_wait(barrier, n_dev - 1)

    n_z = 2 * min(nc, 2)
    z = lax.rem(c, 2) * np_ + p if nc > 1 else p
    ways = []
    for step in (1, n_z - 1):
        to_z = lax.rem(z + step, n_z)
        to_c = c // 2 * 2 + to_z // np_ if nc > 1 else c
        ways.append(r * ncp + to_c * np_ + lax.rem(to_z, np_))

    def give(first, count, sem):
        cut = count // 32 * 16
        both = []
        for k, (at, n) in enumerate(((first, cut), (first + cut, count - cut))):
            rows = pl.ds(at, n)
            both.append(copy(w_send.at[rows], wall.at[p, rows], sem + k, ways[k]))
            both[k].start()
        return both

    early = give(0, n_first, 8)
    send_half(send_out, recv_out, 2, p)
    for w_copy in early:
        w_copy.wait()
    out_half(1 - p)
    send_half(send_out, recv_out, 2, 1 - p)
    late = give(n_first, w_send.shape[0] - n_first, 18)

    def send_rows(s, carry):
        to_cp = lax.rem(cp + s, ncp)
        copy(
            xs.at[pl.ds(to_cp * ROWS, ROWS)], xr.at[:, pl.ds(cp * block_j, block_j), :], 1,
            r * ncp + to_cp,
        ).start()
        return carry

    lax.fori_loop(1, ncp, send_rows, 0)
    xr[:, pl.ds(cp * block_j, block_j), :] = xs[pl.ds(cp * ROWS, ROWS)]
    recv_out[pl.ds(me, 1)] = send_out[pl.ds(slot, 1)]

    def load_rows():
        for w_copy in late:
            w_copy.wait()
        for t in range(3):
            whole = jnp.concatenate(
                [wall[h, base + t * half : base + (t + 1) * half] for h in range(2)], axis=0
            )
            w_fin[t] = whole.astype(F32).T.astype(BF)
        w_bias[...] = jnp.concatenate(
            [wall[h, base + 3 * half : base + 3 * half + 16].astype(F32)[:part] for h in range(2)]
            + [jnp.zeros((8 - heads, n_ch), F32)],
            axis=0,
        ).astype(BF)
        drain(xs.at[pl.ds(0, (ncp - 1) * ROWS)], recv_sem.at[1])

        def load_state(t):
            at = span(t, width)
            row, off = t // (TILES // ROWS), t % (TILES // ROWS)
            tile = xr[row, span(off, width), :].astype(F32).T
            state[:, at] = tile
            gate[:, at] = jax.nn.sigmoid(dot(w_gate[0], norm_columns(tile).astype(BF), (1, 0)))

        steps(TILES, load_state)

    def unpack(load, dst):
        n = n_dev // 8

        def body(t):
            tile = load(t, n).astype(F32).reshape(n * q_rows, lanes)
            dst[span(t, n * q_rows), :] = tile

        steps(8, body)

    def arrived(dst, sem):
        drain(dst.at[pl.ds(0, n_dev - 1)], recv_sem.at[sem])

    def update(t, which):
        at = span(t, width)
        hidden = jnp.concatenate(
            [st_a[pl.ds(t * per + k, n_ch, stride=q_rows), :] for k in range(per)], axis=1
        ).astype(BF)
        step = gate[:, at] * dot(w_fin[which], hidden, (1, 0))
        new = state[:, at] + step
        state[:, at] = new
        delta[:, at] = delta[:, at] + step if which else step
        return new

    def mix_and_return(arm_chunk, back, home, sem, meanwhile):
        n = n_tok // 4
        n_to = n_dev // 4
        y, x, z_of = r // 2, c // np_, lax.rem(c, 2) * np_ + p
        for k in range(4):
            ahead = lax.rem(k + x + z_of, 4)
            m = lax.rem(jnp.where(lax.rem(y, 2) == 0, y + ahead, y + 4 - ahead), 4)
            mixed = dot(arm_chunk(m), arm_b[...], (0, 0))
            for g in range(GROUPS):
                rows = pl.ds(m * (n * GROUPS) + g, n, stride=GROUPS)
                st_c[rows, :] = mixed[:, g * lanes : (g + 1) * lanes]

            def store_back(at, tile):
                back[at] = tile

            pack(st_c, m * n_to, n_to, store_back)

            def body(s, carry, m=m):
                to = m * n_to + lax.rem(me + s * STEP, n_to)
                copy(back.at[to], home.at[slot], sem, to).start()
                return carry

            lax.fori_loop(1, n_to, body, 0)

            @pl.when(m != y)
            def _(body=body):
                body(0, 0)

        home[pl.ds(slot, 1)] = back[pl.ds(me, 1)]
        meanwhile()
        arrived(home, sem)
        m = n_dev // 8

        def sums(t, carry):
            tile = home[pl.ds(t * m, m)].astype(F32)
            return carry[0] + jnp.sum(tile, axis=0), carry[1] + jnp.sum(tile * tile, axis=0)

        zero = jnp.zeros((q_rows, lanes), F32)
        total, squares = zero, zero
        for t in range(8):
            total, squares = sums(t, (total, squares))
        mean = total / n_ch
        scale = lax.rsqrt(squares / n_ch - mean * mean + EPS)

        def normalize(t):
            tile = (home[pl.ds(t * m, m)].astype(F32) - mean[None]) * scale[None]
            st_a[span(t, m * q_rows), :] = tile.reshape(m * q_rows, lanes)

        steps(8, normalize)

    arrived(recv_out, 2)
    left = lax.broadcasted_iota(jnp.int32, (ncp * q_rows, lanes), 1) < block_i

    def lay_out(m, a):
        tiles = [
            recv_out[pl.ds((2 * m + k) * ncp, ncp), a].astype(F32).reshape(ncp * q_rows, lanes)
            for k in range(2)
        ]
        low = jnp.where(left, tiles[0], pltpu.roll(tiles[1], block_i, 1))
        high = jnp.where(left, pltpu.roll(tiles[0], block_i, 1), tiles[1])
        both = [y.reshape(ncp, 1, q_rows, lanes) for y in (low, high)]
        return jnp.concatenate(both, axis=1).reshape(n_tok, lanes).astype(BF)

    for m in range(4):
        arm_b[:, m * lanes : (m + 1) * lanes] = lay_out(m, 1)
    mix_and_return(lambda m: lay_out(m, 0), back_out, home_out, 3, load_rows)

    def in_half(h, first):
        w = wall[pl.ds(h, 1), n_first : 2 * n_first, :].reshape(n_first, n_ch)

        def body(t):
            if first:
                tile = norm_columns(update(t, 0)).astype(BF)
                normed[:, span(t, width)] = tile
            else:
                tile = normed[:, span(t, width)]
            put_arms(w, h, tile, mask_at(mask_r, t), t)

        steps(TILES, body)
        pack_arms(send_in, h * half, half)
        send_half(send_in, recv_in, 4, h)

    in_half(0, True)
    in_half(1, False)
    recv_in[pl.ds(me, 1)] = send_in[pl.ds(slot, 1)]

    def gate_in(t):
        at = span(t, width)
        gate[:, at] = jax.nn.sigmoid(dot(w_gate[1], normed[:, at], (1, 0)))

    steps(TILES, gate_in)
    arrived(recv_in, 4)
    unpack(lambda t, n: recv_in[pl.ds(t * n, n), 0], st_a)
    unpack(lambda t, n: recv_in[pl.ds(t * n, n), 1], st_b)
    for g in range(GROUPS):
        rows = pl.ds(g, n_tok, stride=GROUPS)
        arm_a[:, g * lanes : (g + 1) * lanes] = st_a[rows, :].astype(BF)
        arm_b[:, g * lanes : (g + 1) * lanes] = st_b[rows, :].astype(BF)
    mix_and_return(lambda m: arm_a[:, span(m, lanes)], back_in, home_in, 5, lambda: None)

    def bias_step(t):
        tile = norm_columns(update(t, 1)).astype(BF)
        normed[:, span(t, width)] = tile
        proj = dot(w_bias[...], tile, (1, 0)) * LOG2E
        for k in range(per):
            bias_st[pl.ds(t * per + k, 8, stride=q_rows), :] = proj[:, k * lanes : (k + 1) * lanes]

    steps(TILES, bias_step)
    bias_send[...] = bias_st[: heads * q_rows].astype(BF).reshape(heads, q_rows, lanes)
    for h in range(heads):

        def send_bias(s, carry, h=h):
            other = lax.rem(unit + s * STEP, hdev)
            to = ((other // ncp) * 2 + core) * ncp + lax.rem(other, ncp)
            copy(bias_send.at[h], bias_recv.at[h, core, unit], 10 + h, to).start()
            return carry

        lax.fori_loop(1, hdev, send_bias, 0)
        bias_recv[h, pl.ds(core, 1), pl.ds(unit, 1)] = bias_send[h][None, None]

    def qkvg(t):
        at = span(t, width)
        tile = normed[:, at]
        row, off = t // (TILES // ROWS), t % (TILES // ROWS)
        keys = []
        m = half
        for h in range(2):
            proj = dot(wall[h, 2 * n_first : 3 * n_first], tile, (1, 0))
            mine = slice(h * m, (h + 1) * m)
            q_t[mine, at] = (proj[:m] * (LOG2E * h_dim**-0.5)).astype(BF)
            keys.append(proj[m : 2 * m])
            v_t[mine, at] = proj[2 * m : 3 * m].astype(BF)
            gate[mine, at] = jax.nn.sigmoid(proj[3 * m :])
        k_n[row, span(off, width), :] = jnp.concatenate(keys, axis=0).T.astype(BF)

    steps(TILES, qkvg)
    sibling = (r + 1 - 2 * core) * ncp + cp
    def forward(h):
        drain(bias_recv.at[h, 0, pl.ds(0, hdev - 1)], recv_sem.at[10 + h])
        out = copy(bias_recv.at[h, core], bias_recv.at[h, core], 14 + h, sibling)
        out.start()
        return out

    def finish(i):
        for t in range(TILES // ROWS):
            at = slice(i * n_tok + t * width, i * n_tok + (t + 1) * width)
            gated = (gate[:, at] * att[:, at]).astype(BF)
            total = delta[:, at] + dot(w_fin[2], gated, (1, 0))
            fin_send[i, t * width : (t + 1) * width, :] = total.T.astype(BF)

        def send_final(s, carry):
            to_cp = lax.rem(cp + s, ncp)
            copy(
                fin_send.at[i, pl.ds(to_cp * block_j, block_j), :],
                fin_recv.at[cp * ROWS + i], 7, r * ncp + to_cp,
            ).start()
            return carry

        lax.fori_loop(1, ncp, send_final, 0)

    def attend(h):
        def load(t, n):
            return bias_recv[h, pl.ds(t % 2, 1), pl.ds(t // 2 * n, n)].reshape(n, q_rows, lanes)

        unpack(load, st_a)
        for g in range(GROUPS):
            tile = st_a[pl.ds(g, n_tok, stride=GROUPS), :]
            seen = tm_ref[:, g * lanes : (g + 1) * lanes] > 0
            bias_t[g * lanes : (g + 1) * lanes, :] = jnp.where(seen, tile, -1e30).T
        mine = slice(h * h_dim, (h + 1) * h_dim)

        channel = lax.broadcasted_iota(jnp.int32, (n_ch, n_tok), 0)
        chosen = (channel >= h * h_dim) & (channel < (h + 1) * h_dim)

        def scores_of(i):
            query = q_t[:, i * n_tok : (i + 1) * n_tok].astype(F32)
            return dot(k_n[i], jnp.where(chosen, query, 0.0).astype(BF), (1, 0)) + bias_t[...]

        following = scores_of(0)
        for i in range(ROWS):
            scores = following
            if i + 1 < ROWS:
                following = scores_of(i + 1)
            at = slice(i * n_tok, (i + 1) * n_tok)
            vals = jnp.concatenate([v_t[mine, at], jnp.ones((16, n_tok), BF)], axis=0)
            peak = jnp.max(scores, axis=0, keepdims=True)
            got = dot(vals, jnp.exp2(scores - peak).astype(BF), (1, 0))
            att[mine, at] = got[:h_dim] / got[h_dim : h_dim + 1]
            if h == heads - 1:
                finish(i)

    forwards = [forward(0)]
    for h in range(heads):
        if h + 1 < heads:
            forwards.append(forward(h + 1))
        forwards[h].wait_recv()
        attend(h)

    fin_recv[pl.ds(cp * ROWS, ROWS)] = fin_send[:, pl.ds(cp * block_j, block_j), :]
    drain(fin_recv.at[pl.ds(0, (ncp - 1) * ROWS)], recv_sem.at[7])
    out_ref[...] = fin_recv[...]

    drain(xs.at[pl.ds(0, (ncp - 1) * ROWS)], send_sem.at[1])
    drain(send_out.at[pl.ds(0, n_dev - 1)], send_sem.at[2])
    drain(back_out.at[pl.ds(0, n_dev - 1)], send_sem.at[3])
    drain(send_in.at[pl.ds(0, n_dev - 1)], send_sem.at[4])
    drain(back_in.at[pl.ds(0, n_dev - 1)], send_sem.at[5])
    drain(fin_recv.at[pl.ds(0, (ncp - 1) * ROWS)], send_sem.at[7])
    for h in range(heads):
        drain(bias_recv.at[h, 0, pl.ds(0, hdev - 1)], send_sem.at[10 + h])
        forwards[h].wait_send()


def on_device(
    sizes, pair_input, token_mask,
    out_stack, out_gate, out_final, in_stack, in_gate, in_final, att_stack, att_bias, att_out,
):
    nr, nc, np_ = sizes
    heads = att_bias.shape[1] * np_
    n_dev = nr * nc * np_
    n_ch = n_dev
    n_tok = ROWS * n_dev
    lanes = n_tok // GROUPS
    q_rows = ROWS * GROUPS
    n_pos = ROWS * n_tok
    vm = pltpu.VMEM
    pair_t = (n_ch, n_pos)
    stage = (n_dev * q_rows, lanes)
    two = (n_dev, 2, q_rows, lanes)
    one = (n_dev, q_rows, lanes)
    w_rows = 15 * (n_ch // 2) + 16
    update = pl.pallas_call(
        functools.partial(kernel, (nr, nc, np_, heads)),
        out_shape=jax.ShapeDtypeStruct(pair_input.shape, BF),
        in_specs=[pl.BlockSpec(memory_space=pltpu.VMEM)] * 11,
        out_specs=pl.BlockSpec(memory_space=pltpu.VMEM),
        scratch_shapes=[
            vm((w_rows, n_ch), BF),
            vm((2, w_rows, n_ch), BF),
            vm((2, n_ch, n_ch), BF),
            vm((8, n_ch), BF),
            vm((3, n_ch, n_ch), BF),
            vm((q_rows, lanes), F32),
            vm((q_rows, lanes), F32),
            vm(pair_input.shape, BF),
            vm((ROWS, n_tok, n_ch), BF),
            vm(pair_t, F32),
            vm(pair_t, F32),
            vm(pair_t, F32),
            vm(stage, F32),
            vm(stage, F32),
            vm(stage, F32),
            vm(two, BF), vm(two, BF), vm(one, BF), vm(one, BF),
            vm(two, BF), vm(two, BF), vm(one, BF), vm(one, BF),
            vm((n_tok, n_tok), BF),
            vm((n_tok, n_tok), BF),
            vm(pair_t, BF),
            vm((8 * q_rows, lanes), F32),
            vm((heads, q_rows, lanes), BF),
            vm((heads, 2, n_dev // 2, q_rows, lanes), BF),
            vm((n_tok, n_tok), F32),
            vm(pair_t, BF),
            vm((ROWS, n_tok, n_ch), BF),
            vm(pair_t, BF),
            vm(pair_t, F32),
            vm((ROWS, n_tok, n_ch), BF),
            vm(pair_input.shape, BF),
            pltpu.SemaphoreType.DMA((20,)),
            pltpu.SemaphoreType.DMA((20,)),
        ],
        compiler_params=pltpu.CompilerParams(
            collective_id=0, has_side_effects=True, vmem_limit_bytes=56 * 2**20
        ),
        name="pair_update",
    )(
        pair_input, token_mask[None, :],
        jnp.swapaxes(out_stack, 1, 2), jnp.swapaxes(in_stack, 1, 2), jnp.swapaxes(att_stack, 1, 2),
        out_final, in_final, att_out, att_bias.T, out_gate, in_gate,
    )
    return pair_input + update.astype(F32)


def solution(mesh):
    sizes = tuple(mesh.shape[name] for name in ("row", "col", "chip"))
    return jax.shard_map(
        functools.partial(on_device, sizes),
        mesh=mesh,
        in_specs=(
            P("row", ("col", "chip"), None),
            P(),
            P(None, None, "chip"),
            P(),
            P("chip", None),
            P(None, None, "chip"),
            P(),
            P("chip", None),
            P(None, None, "chip"),
            P(None, "chip"),
            P("chip", None),
        ),
        out_specs=P("row", ("col", "chip"), None),
        check_vma=False,
    )
```

```python
import functools
import math

import jax
import jax.numpy as jnp
from jax import lax
from jax.experimental import pallas as pl
from jax.experimental.pallas import tpu as pltpu
from jax.sharding import PartitionSpec as P

EPS = 1e-05
LOG2E = math.log2(math.e)
MESH = pl.DeviceIdType.MESH
BF = jnp.bfloat16
F32 = jnp.float32
ROWS = 4
GROUPS = 4
TILES = 8
STEP = 21


def dot(a, b, contract):
    return lax.dot_general(a, b, ((contract[:1], contract[1:]), ((), ())), preferred_element_type=F32)


def steps(count, body):
    for t in range(count):
        body(t)


def norm_columns(x):
    mean = jnp.mean(x, axis=0, keepdims=True)
    square = jnp.mean(x * x, axis=0, keepdims=True)
    return (x - mean) * lax.rsqrt(square - mean * mean + EPS)


def kernel(
    sizes,
    x_ref, tm_ref, os_ref, is_ref, as_ref, of_ref, if_ref, ao_ref, ab_ref, og_ref, ig_ref,
    out_ref,
    w_send, wall, w_gate, w_bias, w_fin, mask_o, mask_r,
    xs, xr, state, delta, gate, st_a, st_b, st_c,
    send_out, recv_out, back_out, home_out,
    send_in, recv_in, back_in, home_in,
    arm_a, arm_b,
    normed, bias_st, bias_send, bias_recv, bias_t,
    q_t, k_n, v_t, att, fin_send, fin_recv,
    send_sem, recv_sem,
):
    nr, nc, np_, heads = sizes
    ncp = nc * np_
    n_dev = nr * ncp
    n_ch = n_dev
    half = n_ch // 2
    hdev = n_dev // 2
    n_tok = ROWS * n_dev
    lanes = n_tok // GROUPS
    q_rows = ROWS * GROUPS
    n_pos = ROWS * n_tok
    width = n_pos // TILES
    per = width // lanes
    block_i = n_tok // nr
    block_j = n_tok // ncp
    h_dim = n_ch // heads
    r, c, p = lax.axis_index("row"), lax.axis_index("col"), lax.axis_index("chip")
    cp = c * np_ + p
    me = r * ncp + cp
    core, unit = lax.rem(r, 2), (r // 2) * ncp + cp
    slot = core * hdev + unit

    barrier = pltpu.get_barrier_semaphore()

    def place(to):
        return lax.div(to, ncp), lax.div(lax.rem(to, ncp), np_), lax.rem(to, np_)

    def at_unit(other, k):
        col = lax.div(lax.rem(other, ncp), np_)
        return lax.div(other, ncp) * 2 + k, col, lax.rem(other, np_)

    for s in range(1, n_dev):
        s = s * STEP % n_dev
        to_r = lax.rem(r + s // ncp, nr)
        to = (to_r, lax.rem(c + s % ncp // np_, nc), lax.rem(p + s % np_, np_))
        pl.semaphore_signal(barrier, inc=1, device_id=to, device_id_type=MESH)

    def copy(src, dst, sem, to):
        return pltpu.make_async_remote_copy(
            src_ref=src, dst_ref=dst, send_sem=send_sem.at[sem], recv_sem=recv_sem.at[sem],
            device_id=to if isinstance(to, tuple) else place(to), device_id_type=MESH,
        )

    def drain(ref, sem):
        pltpu.make_async_copy(ref, ref, sem).wait()

    def span(t, size):
        at = t * size
        return pl.ds(at if isinstance(at, int) else pl.multiple_of(at, size), size)

    n_first = 4 * half
    base = 3 * n_first
    for t, ref in enumerate((os_ref, is_ref, as_ref)):
        for s in range(4):
            rows = pl.ds((4 * t + s) * half, half)
            w_send[rows, :] = ref[s]
    for t, ref in enumerate((of_ref, if_ref, ao_ref)):
        w_send[base + t * half : base + (t + 1) * half, :] = ref[...]
    part = heads // 2
    w_send[base + 3 * half :, :] = jnp.concatenate(
        [ab_ref[...].astype(F32), jnp.zeros((16 - part, n_ch), F32)], axis=0
    ).astype(BF)
    wall[pl.ds(p, 1)] = w_send[...][None]
    for t, ref in enumerate((og_ref, ig_ref)):
        w_gate[t] = ref[...].astype(F32).T.astype(BF)

    live = tm_ref[...].astype(F32)
    token = lax.broadcasted_iota(jnp.int32, (lanes, n_tok), 1)
    lane = lax.broadcasted_iota(jnp.int32, (lanes, n_tok), 0)
    live_b = jnp.broadcast_to(live, (lanes, n_tok)).astype(BF)
    pick = (token == r * block_i + lax.rem(lane, block_i)).astype(F32).astype(BF)
    by_i = dot(live_b[:q_rows], pick, (1, 1))
    row_q = lax.broadcasted_iota(jnp.int32, (q_rows, n_tok), 0)
    token_q = lax.broadcasted_iota(jnp.int32, (q_rows, n_tok), 1)
    by_j = [
        dot((token_q == cp * block_j + e * q_rows + row_q).astype(F32).astype(BF), live_b, (1, 1))
        for e in range(2)
    ]
    lane_q = lax.broadcasted_iota(jnp.int32, (q_rows, lanes), 1)
    mask_o[...] = jnp.where(lane_q < block_i, by_j[0], by_j[1]) * by_i
    own = dot((token_q == me * ROWS + row_q // GROUPS).astype(F32).astype(BF), live_b, (1, 1))
    wide_live = jnp.concatenate(
        [live[:, g * lanes : (g + 1) * lanes] for g in range(GROUPS)] * ROWS, axis=0
    )
    mask_r[...] = own * wide_live

    xs[...] = x_ref[...].astype(BF)
    st_a[...] = x_ref[...].reshape(block_i * block_j, n_ch)

    def norm_input(t):
        tile = jnp.concatenate(
            [
                st_a[pl.ds(e * q_rows + t * per + k, block_i, stride=block_j), :]
                for k in range(per)
                for e in range(2)
            ],
            axis=0,
        )
        normed[:, span(t, width)] = norm_columns(tile.T).astype(BF)

    steps(TILES, norm_input)

    def put_arms(w, h, tile, mask, t):
        proj = dot(w, tile, (1, 0))
        m = half
        first = jax.nn.sigmoid(proj[:m]) * proj[m : 2 * m] * mask
        second = jax.nn.sigmoid(proj[2 * m : 3 * m]) * proj[3 * m :] * mask
        for k in range(per):
            rows = pl.ds(h * (half * q_rows) + t * per + k, half, stride=q_rows)
            st_b[rows, :] = first[:, k * lanes : (k + 1) * lanes]
            st_c[rows, :] = second[:, k * lanes : (k + 1) * lanes]

    def mask_at(ref, t):
        return jnp.concatenate([ref[pl.ds(t * per + k, 1), :] for k in range(per)], axis=1)

    def pack(src, first, count, store):
        n = max(count // 8, 1)

        def body(t):
            at = first + t * n
            start = at * q_rows
            if not isinstance(at, int):
                start = pl.multiple_of(start, n * q_rows)
            rows = pl.ds(start, n * q_rows)
            store(pl.ds(at, n), src[rows, :].reshape(n, q_rows, lanes).astype(BF))

        steps(count // n, body)

    def pack_arms(send, first, count):
        def store_first(at, tile):
            send[at, 0] = tile

        def store_second(at, tile):
            send[at, 1] = tile

        pack(st_b, first, count, store_first)
        pack(st_c, first, count, store_second)

    def out_half(h):
        w = wall[pl.ds(h, 1), :n_first, :].reshape(n_first, n_ch)

        def body(t):
            put_arms(w, h, normed[:, span(t, width)], mask_at(mask_o, t), t)

        steps(TILES, body)
        pack_arms(send_out, h * half, half)

    def send_half(send, recv, sem, h):
        def body(s, carry):
            other = lax.rem(unit + s * STEP, hdev)
            copy(send.at[h * hdev + other], recv.at[me], sem, at_unit(other, h)).start()
            return carry

        lax.fori_loop(1, hdev, body, 0)

        @pl.when(core != h)
        def _():
            body(0, 0)

    out_half(p)
    pl.semaphore_wait(barrier, n_dev - 1)

    n_z = 2 * min(nc, 2)
    z = lax.rem(c, 2) * np_ + p if nc > 1 else p
    ways = []
    for step in (1, n_z - 1):
        to_z = lax.rem(z + step, n_z)
        to_c = c // 2 * 2 + to_z // np_ if nc > 1 else c
        ways.append(r * ncp + to_c * np_ + lax.rem(to_z, np_))

    def give(first, count, sem):
        cut = count // 32 * 16
        both = []
        for k, (at, n) in enumerate(((first, cut), (first + cut, count - cut))):
            rows = pl.ds(at, n)
            both.append(copy(w_send.at[rows], wall.at[p, rows], sem + k, ways[k]))
            both[k].start()
        return both

    early = give(0, n_first, 8)
    send_half(send_out, recv_out, 2, p)
    for w_copy in early:
        w_copy.wait()
    out_half(1 - p)
    send_half(send_out, recv_out, 2, 1 - p)
    late = give(n_first, w_send.shape[0] - n_first, 18)

    def send_rows(s, carry):
        to_cp = lax.rem(cp + s, ncp)
        copy(
            xs.at[pl.ds(to_cp * ROWS, ROWS)], xr.at[:, pl.ds(cp * block_j, block_j), :], 1,
            r * ncp + to_cp,
        ).start()
        return carry

    lax.fori_loop(1, ncp, send_rows, 0)
    xr[:, pl.ds(cp * block_j, block_j), :] = xs[pl.ds(cp * ROWS, ROWS)]
    recv_out[pl.ds(me, 1)] = send_out[pl.ds(slot, 1)]

    def load_rows():
        for w_copy in late:
            w_copy.wait()
        for t in range(3):
            whole = jnp.concatenate(
                [wall[h, base + t * half : base + (t + 1) * half] for h in range(2)], axis=0
            )
            w_fin[t] = whole.astype(F32).T.astype(BF)
        w_bias[...] = jnp.concatenate(
            [wall[h, base + 3 * half : base + 3 * half + 16].astype(F32)[:part] for h in range(2)]
            + [jnp.zeros((8 - heads, n_ch), F32)],
            axis=0,
        ).astype(BF)
        drain(xs.at[pl.ds(0, (ncp - 1) * ROWS)], recv_sem.at[1])

        def load_state(t):
            at = span(t, width)
            row, off = t // (TILES // ROWS), t % (TILES // ROWS)
            tile = xr[row, span(off, width), :].astype(F32).T
            state[:, at] = tile
            gate[:, at] = jax.nn.sigmoid(dot(w_gate[0], norm_columns(tile).astype(BF), (1, 0)))

        steps(TILES, load_state)

    def unpack(load, dst):
        n = n_dev // 8

        def body(t):
            tile = load(t, n).astype(F32).reshape(n * q_rows, lanes)
            dst[span(t, n * q_rows), :] = tile

        steps(8, body)

    def arrived(dst, sem):
        drain(dst.at[pl.ds(0, n_dev - 1)], recv_sem.at[sem])

    def update(t, which):
        at = span(t, width)
        hidden = jnp.concatenate(
            [st_a[pl.ds(t * per + k, n_ch, stride=q_rows), :] for k in range(per)], axis=1
        ).astype(BF)
        step = gate[:, at] * dot(w_fin[which], hidden, (1, 0))
        new = state[:, at] + step
        state[:, at] = new
        delta[:, at] = delta[:, at] + step if which else step
        return new

    def mix_and_return(arm_chunk, back, home, sem, meanwhile):
        n = n_tok // 4
        n_to = n_dev // 4
        y, x, z_of = r // 2, c // np_, lax.rem(c, 2) * np_ + p
        for k in range(4):
            ahead = lax.rem(k + x + z_of, 4)
            m = lax.rem(jnp.where(lax.rem(y, 2) == 0, y + ahead, y + 4 - ahead), 4)
            mixed = dot(arm_chunk(m), arm_b[...], (0, 0))
            for g in range(GROUPS):
                rows = pl.ds(m * (n * GROUPS) + g, n, stride=GROUPS)
                st_c[rows, :] = mixed[:, g * lanes : (g + 1) * lanes]

            def store_back(at, tile):
                back[at] = tile

            pack(st_c, m * n_to, n_to, store_back)

            def body(s, carry, m=m):
                to = m * n_to + lax.rem(me + s * STEP, n_to)
                copy(back.at[to], home.at[slot], sem, to).start()
                return carry

            lax.fori_loop(1, n_to, body, 0)

            @pl.when(m != y)
            def _(body=body):
                body(0, 0)

        home[pl.ds(slot, 1)] = back[pl.ds(me, 1)]
        meanwhile()
        arrived(home, sem)
        m = n_dev // 8

        def sums(t, carry):
            tile = home[pl.ds(t * m, m)].astype(F32)
            return carry[0] + jnp.sum(tile, axis=0), carry[1] + jnp.sum(tile * tile, axis=0)

        zero = jnp.zeros((q_rows, lanes), F32)
        total, squares = zero, zero
        for t in range(8):
            total, squares = sums(t, (total, squares))
        mean = total / n_ch
        scale = lax.rsqrt(squares / n_ch - mean * mean + EPS)

        def normalize(t):
            tile = (home[pl.ds(t * m, m)].astype(F32) - mean[None]) * scale[None]
            st_a[span(t, m * q_rows), :] = tile.reshape(m * q_rows, lanes)

        steps(8, normalize)

    arrived(recv_out, 2)
    left = lax.broadcasted_iota(jnp.int32, (ncp * q_rows, lanes), 1) < block_i

    def lay_out(m, a):
        tiles = [
            recv_out[pl.ds((2 * m + k) * ncp, ncp), a].astype(F32).reshape(ncp * q_rows, lanes)
            for k in range(2)
        ]
        low = jnp.where(left, tiles[0], pltpu.roll(tiles[1], block_i, 1))
        high = jnp.where(left, pltpu.roll(tiles[0], block_i, 1), tiles[1])
        both = [y.reshape(ncp, 1, q_rows, lanes) for y in (low, high)]
        return jnp.concatenate(both, axis=1).reshape(n_tok, lanes).astype(BF)

    for m in range(4):
        arm_b[:, m * lanes : (m + 1) * lanes] = lay_out(m, 1)
    mix_and_return(lambda m: lay_out(m, 0), back_out, home_out, 3, load_rows)

    def in_half(h, first):
        w = wall[pl.ds(h, 1), n_first : 2 * n_first, :].reshape(n_first, n_ch)

        def body(t):
            if first:
                tile = norm_columns(update(t, 0)).astype(BF)
                normed[:, span(t, width)] = tile
            else:
                tile = normed[:, span(t, width)]
            put_arms(w, h, tile, mask_at(mask_r, t), t)

        steps(TILES, body)
        pack_arms(send_in, h * half, half)
        send_half(send_in, recv_in, 4, h)

    in_half(0, True)
    in_half(1, False)
    recv_in[pl.ds(me, 1)] = send_in[pl.ds(slot, 1)]

    def gate_in(t):
        at = span(t, width)
        gate[:, at] = jax.nn.sigmoid(dot(w_gate[1], normed[:, at], (1, 0)))

    steps(TILES, gate_in)
    arrived(recv_in, 4)
    unpack(lambda t, n: recv_in[pl.ds(t * n, n), 0], st_a)
    unpack(lambda t, n: recv_in[pl.ds(t * n, n), 1], st_b)
    for g in range(GROUPS):
        rows = pl.ds(g, n_tok, stride=GROUPS)
        arm_a[:, g * lanes : (g + 1) * lanes] = st_a[rows, :].astype(BF)
        arm_b[:, g * lanes : (g + 1) * lanes] = st_b[rows, :].astype(BF)
    mix_and_return(lambda m: arm_a[:, span(m, lanes)], back_in, home_in, 5, lambda: None)

    def bias_step(t):
        tile = norm_columns(update(t, 1)).astype(BF)
        normed[:, span(t, width)] = tile
        proj = dot(w_bias[...], tile, (1, 0)) * LOG2E
        for k in range(per):
            bias_st[pl.ds(t * per + k, 8, stride=q_rows), :] = proj[:, k * lanes : (k + 1) * lanes]

    steps(TILES, bias_step)
    bias_send[...] = bias_st[: heads * q_rows].astype(BF).reshape(heads, q_rows, lanes)
    for h in range(heads):

        def send_bias(s, carry, h=h):
            other = lax.rem(unit + s * STEP, hdev)
            copy(bias_send.at[h], bias_recv.at[h, core, unit], 10 + h, at_unit(other, core)).start()
            return carry

        lax.fori_loop(1, hdev, send_bias, 0)
        bias_recv[h, pl.ds(core, 1), pl.ds(unit, 1)] = bias_send[h][None, None]

    def qkvg(t):
        at = span(t, width)
        tile = normed[:, at]
        row, off = t // (TILES // ROWS), t % (TILES // ROWS)
        keys = []
        m = half
        for h in range(2):
            proj = dot(wall[h, 2 * n_first : 3 * n_first], tile, (1, 0))
            mine = slice(h * m, (h + 1) * m)
            q_t[mine, at] = (proj[:m] * (LOG2E * h_dim**-0.5)).astype(BF)
            keys.append(proj[m : 2 * m])
            v_t[mine, at] = proj[2 * m : 3 * m].astype(BF)
            gate[mine, at] = jax.nn.sigmoid(proj[3 * m :])
        k_n[row, span(off, width), :] = jnp.concatenate(keys, axis=0).T.astype(BF)

    steps(TILES, qkvg)
    sibling = (r + 1 - 2 * core) * ncp + cp
    def forward(h):
        drain(bias_recv.at[h, 0, pl.ds(0, hdev - 1)], recv_sem.at[10 + h])
        out = copy(bias_recv.at[h, core], bias_recv.at[h, core], 14 + h, sibling)
        out.start()
        return out

    def finish(i):
        for t in range(TILES // ROWS):
            at = slice(i * n_tok + t * width, i * n_tok + (t + 1) * width)
            gated = (gate[:, at] * att[:, at]).astype(BF)
            total = delta[:, at] + dot(w_fin[2], gated, (1, 0))
            fin_send[i, t * width : (t + 1) * width, :] = total.T.astype(BF)

        def send_final(s, carry):
            to_cp = lax.rem(cp + s, ncp)
            copy(
                fin_send.at[i, pl.ds(to_cp * block_j, block_j), :],
                fin_recv.at[cp * ROWS + i], 7, r * ncp + to_cp,
            ).start()
            return carry

        lax.fori_loop(1, ncp, send_final, 0)

    def attend(h):
        def load(t, n):
            return bias_recv[h, pl.ds(t % 2, 1), pl.ds(t // 2 * n, n)].reshape(n, q_rows, lanes)

        unpack(load, st_a)
        for g in range(GROUPS):
            tile = st_a[pl.ds(g, n_tok, stride=GROUPS), :]
            seen = tm_ref[:, g * lanes : (g + 1) * lanes] > 0
            bias_t[g * lanes : (g + 1) * lanes, :] = jnp.where(seen, tile, -1e30).T
        mine = slice(h * h_dim, (h + 1) * h_dim)

        channel = lax.broadcasted_iota(jnp.int32, (n_ch, n_tok), 0)
        chosen = (channel >= h * h_dim) & (channel < (h + 1) * h_dim)

        def scores_of(i):
            query = q_t[:, i * n_tok : (i + 1) * n_tok].astype(F32)
            return dot(k_n[i], jnp.where(chosen, query, 0.0).astype(BF), (1, 0)) + bias_t[...]

        following = scores_of(0)
        for i in range(ROWS):
            scores = following
            if i + 1 < ROWS:
                following = scores_of(i + 1)
            at = slice(i * n_tok, (i + 1) * n_tok)
            vals = jnp.concatenate([v_t[mine, at], jnp.ones((16, n_tok), BF)], axis=0)
            peak = jnp.max(scores, axis=0, keepdims=True)
            got = dot(vals, jnp.exp2(scores - peak).astype(BF), (1, 0))
            att[mine, at] = got[:h_dim] / got[h_dim : h_dim + 1]
            if h == heads - 1:
                finish(i)

    forwards = [forward(0)]
    for h in range(heads):
        if h + 1 < heads:
            forwards.append(forward(h + 1))
        forwards[h].wait_recv()
        attend(h)

    fin_recv[pl.ds(cp * ROWS, ROWS)] = fin_send[:, pl.ds(cp * block_j, block_j), :]
    drain(fin_recv.at[pl.ds(0, (ncp - 1) * ROWS)], recv_sem.at[7])
    out_ref[...] = fin_recv[...]

    drain(xs.at[pl.ds(0, (ncp - 1) * ROWS)], send_sem.at[1])
    drain(send_out.at[pl.ds(0, n_dev - 1)], send_sem.at[2])
    drain(back_out.at[pl.ds(0, n_dev - 1)], send_sem.at[3])
    drain(send_in.at[pl.ds(0, n_dev - 1)], send_sem.at[4])
    drain(back_in.at[pl.ds(0, n_dev - 1)], send_sem.at[5])
    drain(fin_recv.at[pl.ds(0, (ncp - 1) * ROWS)], send_sem.at[7])
    for h in range(heads):
        drain(bias_recv.at[h, 0, pl.ds(0, hdev - 1)], send_sem.at[10 + h])
        forwards[h].wait_send()


def on_device(
    sizes, pair_input, token_mask,
    out_stack, out_gate, out_final, in_stack, in_gate, in_final, att_stack, att_bias, att_out,
):
    nr, nc, np_ = sizes
    heads = att_bias.shape[1] * np_
    n_dev = nr * nc * np_
    n_ch = n_dev
    n_tok = ROWS * n_dev
    lanes = n_tok // GROUPS
    q_rows = ROWS * GROUPS
    n_pos = ROWS * n_tok
    vm = pltpu.VMEM
    pair_t = (n_ch, n_pos)
    stage = (n_dev * q_rows, lanes)
    two = (n_dev, 2, q_rows, lanes)
    one = (n_dev, q_rows, lanes)
    w_rows = 15 * (n_ch // 2) + 16
    update = pl.pallas_call(
        functools.partial(kernel, (nr, nc, np_, heads)),
        out_shape=jax.ShapeDtypeStruct(pair_input.shape, BF),
        in_specs=[pl.BlockSpec(memory_space=pltpu.VMEM)] * 11,
        out_specs=pl.BlockSpec(memory_space=pltpu.VMEM),
        scratch_shapes=[
            vm((w_rows, n_ch), BF),
            vm((2, w_rows, n_ch), BF),
            vm((2, n_ch, n_ch), BF),
            vm((8, n_ch), BF),
            vm((3, n_ch, n_ch), BF),
            vm((q_rows, lanes), F32),
            vm((q_rows, lanes), F32),
            vm(pair_input.shape, BF),
            vm((ROWS, n_tok, n_ch), BF),
            vm(pair_t, F32),
            vm(pair_t, F32),
            vm(pair_t, F32),
            vm(stage, F32),
            vm(stage, F32),
            vm(stage, F32),
            vm(two, BF), vm(two, BF), vm(one, BF), vm(one, BF),
            vm(two, BF), vm(two, BF), vm(one, BF), vm(one, BF),
            vm((n_tok, n_tok), BF),
            vm((n_tok, n_tok), BF),
            vm(pair_t, BF),
            vm((8 * q_rows, lanes), F32),
            vm((heads, q_rows, lanes), BF),
            vm((heads, 2, n_dev // 2, q_rows, lanes), BF),
            vm((n_tok, n_tok), F32),
            vm(pair_t, BF),
            vm((ROWS, n_tok, n_ch), BF),
            vm(pair_t, BF),
            vm(pair_t, F32),
            vm((ROWS, n_tok, n_ch), BF),
            vm(pair_input.shape, BF),
            pltpu.SemaphoreType.DMA((20,)),
            pltpu.SemaphoreType.DMA((20,)),
        ],
        compiler_params=pltpu.CompilerParams(
            collective_id=0, has_side_effects=True, vmem_limit_bytes=56 * 2**20
        ),
        name="pair_update",
    )(
        pair_input, token_mask[None, :],
        jnp.swapaxes(out_stack, 1, 2), jnp.swapaxes(in_stack, 1, 2), jnp.swapaxes(att_stack, 1, 2),
        out_final, in_final, att_out, att_bias.T, out_gate, in_gate,
    )
    return pair_input + update.astype(F32)


def solution(mesh):
    sizes = tuple(mesh.shape[name] for name in ("row", "col", "chip"))
    return jax.shard_map(
        functools.partial(on_device, sizes),
        mesh=mesh,
        in_specs=(
            P("row", ("col", "chip"), None),
            P(),
            P(None, None, "chip"),
            P(),
            P("chip", None),
            P(None, None, "chip"),
            P(),
            P("chip", None),
            P(None, None, "chip"),
            P(None, "chip"),
            P("chip", None),
        ),
        out_specs=P("row", ("col", "chip"), None),
        check_vma=False,
    )
```

```python
import functools
import math

import jax
import jax.numpy as jnp
from jax import lax
from jax.experimental import pallas as pl
from jax.experimental.pallas import tpu as pltpu
from jax.sharding import PartitionSpec as P

EPS = 1e-05
LOG2E = math.log2(math.e)
MESH = pl.DeviceIdType.MESH
BF = jnp.bfloat16
F32 = jnp.float32
ROWS = 4
GROUPS = 4
TILES = 8
STEP = 21


def dot(a, b, contract):
    return lax.dot_general(a, b, ((contract[:1], contract[1:]), ((), ())), preferred_element_type=F32)


def steps(count, body):
    for t in range(count):
        body(t)


def norm_columns(x):
    mean = jnp.mean(x, axis=0, keepdims=True)
    square = jnp.mean(x * x, axis=0, keepdims=True)
    return (x - mean) * lax.rsqrt(square - mean * mean + EPS)


def kernel(
    sizes,
    x_ref, tm_ref, os_ref, is_ref, as_ref, of_ref, if_ref, ao_ref, ab_ref, og_ref, ig_ref,
    out_ref,
    w_send, wall, w_gate, w_bias, w_fin, mask_o, mask_r,
    xs, xr, state, delta, gate, st_a, st_b, st_c,
    send_out, recv_out, back_out, home_out,
    send_in, recv_in, back_in, home_in,
    arm_a, arm_b,
    normed, bias_st, bias_send, bias_recv, bias_t,
    q_t, k_n, v_t, att, fin_send, fin_recv,
    send_sem, recv_sem,
):
    nr, nc, np_, heads = sizes
    ncp = nc * np_
    n_dev = nr * ncp
    n_ch = n_dev
    half = n_ch // 2
    hdev = n_dev // 2
    n_tok = ROWS * n_dev
    lanes = n_tok // GROUPS
    q_rows = ROWS * GROUPS
    n_pos = ROWS * n_tok
    width = n_pos // TILES
    per = width // lanes
    block_i = n_tok // nr
    block_j = n_tok // ncp
    h_dim = n_ch // heads
    r, c, p = lax.axis_index("row"), lax.axis_index("col"), lax.axis_index("chip")
    cp = c * np_ + p
    me = r * ncp + cp
    core, unit = lax.rem(r, 2), (r // 2) * ncp + cp
    slot = core * hdev + unit

    barrier = pltpu.get_barrier_semaphore()

    def place(to):
        return lax.div(to, ncp), lax.div(lax.rem(to, ncp), np_), lax.rem(to, np_)

    def at_unit(other, k):
        col = lax.div(lax.rem(other, ncp), np_)
        return lax.div(other, ncp) * 2 + k, col, lax.rem(other, np_)

    for s in range(1, n_dev):
        s = s * STEP % n_dev
        to_r = lax.rem(r + s // ncp, nr)
        to = (to_r, lax.rem(c + s % ncp // np_, nc), lax.rem(p + s % np_, np_))
        pl.semaphore_signal(barrier, inc=1, device_id=to, device_id_type=MESH)

    def copy(src, dst, sem, to):
        return pltpu.make_async_remote_copy(
            src_ref=src, dst_ref=dst, send_sem=send_sem.at[sem], recv_sem=recv_sem.at[sem],
            device_id=to if isinstance(to, tuple) else place(to), device_id_type=MESH,
        )

    def drain(ref, sem):
        pltpu.make_async_copy(ref, ref, sem).wait()

    def span(t, size):
        at = t * size
        return pl.ds(at if isinstance(at, int) else pl.multiple_of(at, size), size)

    n_first = 4 * half
    base = 3 * n_first
    for t, ref in enumerate((os_ref, is_ref, as_ref)):
        for s in range(4):
            rows = pl.ds((4 * t + s) * half, half)
            w_send[rows, :] = ref[s]
    for t, ref in enumerate((of_ref, if_ref, ao_ref)):
        w_send[base + t * half : base + (t + 1) * half, :] = ref[...]
    part = heads // 2
    w_send[base + 3 * half :, :] = jnp.concatenate(
        [ab_ref[...].astype(F32), jnp.zeros((16 - part, n_ch), F32)], axis=0
    ).astype(BF)
    wall[pl.ds(p, 1)] = w_send[...][None]
    for t, ref in enumerate((og_ref, ig_ref)):
        w_gate[t] = ref[...].astype(F32).T.astype(BF)

    live = tm_ref[...].astype(F32)
    token = lax.broadcasted_iota(jnp.int32, (lanes, n_tok), 1)
    lane = lax.broadcasted_iota(jnp.int32, (lanes, n_tok), 0)
    live_b = jnp.broadcast_to(live, (lanes, n_tok)).astype(BF)
    pick = (token == r * block_i + lax.rem(lane, block_i)).astype(F32).astype(BF)
    by_i = dot(live_b[:q_rows], pick, (1, 1))
    row_q = lax.broadcasted_iota(jnp.int32, (q_rows, n_tok), 0)
    token_q = lax.broadcasted_iota(jnp.int32, (q_rows, n_tok), 1)
    by_j = [
        dot((token_q == cp * block_j + e * q_rows + row_q).astype(F32).astype(BF), live_b, (1, 1))
        for e in range(2)
    ]
    lane_q = lax.broadcasted_iota(jnp.int32, (q_rows, lanes), 1)
    mask_o[...] = jnp.where(lane_q < block_i, by_j[0], by_j[1]) * by_i
    own = dot((token_q == me * ROWS + row_q // GROUPS).astype(F32).astype(BF), live_b, (1, 1))
    wide_live = jnp.concatenate(
        [live[:, g * lanes : (g + 1) * lanes] for g in range(GROUPS)] * ROWS, axis=0
    )
    mask_r[...] = own * wide_live

    xs[...] = x_ref[...].astype(BF)
    st_a[...] = x_ref[...].reshape(block_i * block_j, n_ch)

    def norm_input(t):
        tile = jnp.concatenate(
            [
                st_a[pl.ds(e * q_rows + t * per + k, block_i, stride=block_j), :]
                for k in range(per)
                for e in range(2)
            ],
            axis=0,
        )
        normed[:, span(t, width)] = norm_columns(tile.T).astype(BF)

    steps(TILES, norm_input)

    def put_arms(w, h, tile, mask, t):
        proj = dot(w, tile, (1, 0))
        m = half
        first = jax.nn.sigmoid(proj[:m]) * proj[m : 2 * m] * mask
        second = jax.nn.sigmoid(proj[2 * m : 3 * m]) * proj[3 * m :] * mask
        for k in range(per):
            rows = pl.ds(h * (half * q_rows) + t * per + k, half, stride=q_rows)
            st_b[rows, :] = first[:, k * lanes : (k + 1) * lanes]
            st_c[rows, :] = second[:, k * lanes : (k + 1) * lanes]

    def mask_at(ref, t):
        return jnp.concatenate([ref[pl.ds(t * per + k, 1), :] for k in range(per)], axis=1)

    def pack(src, first, count, store):
        n = max(count // 8, 1)

        def body(t):
            at = first + t * n
            start = at * q_rows
            if not isinstance(at, int):
                start = pl.multiple_of(start, n * q_rows)
            rows = pl.ds(start, n * q_rows)
            store(pl.ds(at, n), src[rows, :].reshape(n, q_rows, lanes).astype(BF))

        steps(count // n, body)

    def pack_arms(send, first, count):
        def store_first(at, tile):
            send[at, 0] = tile

        def store_second(at, tile):
            send[at, 1] = tile

        pack(st_b, first, count, store_first)
        pack(st_c, first, count, store_second)

    def out_half(h):
        w = wall[pl.ds(h, 1), :n_first, :].reshape(n_first, n_ch)

        def body(t):
            put_arms(w, h, normed[:, span(t, width)], mask_at(mask_o, t), t)

        steps(TILES, body)
        pack_arms(send_out, h * half, half)

    def send_half(send, recv, sem, h):
        def body(s, carry):
            other = lax.rem(unit + s * STEP, hdev)
            copy(send.at[h * hdev + other], recv.at[me], sem, at_unit(other, h)).start()
            return carry

        lax.fori_loop(1, hdev, body, 0)

        @pl.when(core != h)
        def _():
            body(0, 0)

    out_half(p)
    pl.semaphore_wait(barrier, n_dev - 1)

    n_z = 2 * min(nc, 2)
    z = lax.rem(c, 2) * np_ + p if nc > 1 else p
    ways = []
    for step in (1, n_z - 1):
        to_z = lax.rem(z + step, n_z)
        to_c = c // 2 * 2 + to_z // np_ if nc > 1 else c
        ways.append(r * ncp + to_c * np_ + lax.rem(to_z, np_))

    def give(first, count, sem):
        cut = count // 32 * 16
        both = []
        for k, (at, n) in enumerate(((first, cut), (first + cut, count - cut))):
            rows = pl.ds(at, n)
            both.append(copy(w_send.at[rows], wall.at[p, rows], sem + k, ways[k]))
            both[k].start()
        return both

    early = give(0, n_first, 8)
    send_half(send_out, recv_out, 2, p)
    for w_copy in early:
        w_copy.wait()
    out_half(1 - p)
    send_half(send_out, recv_out, 2, 1 - p)
    late = give(n_first, w_send.shape[0] - n_first, 18)

    def send_rows(s, carry):
        to_cp = lax.rem(cp + s, ncp)
        copy(
            xs.at[pl.ds(to_cp * ROWS, ROWS)], xr.at[:, pl.ds(cp * block_j, block_j), :], 1,
            r * ncp + to_cp,
        ).start()
        return carry

    lax.fori_loop(1, ncp, send_rows, 0)
    xr[:, pl.ds(cp * block_j, block_j), :] = xs[pl.ds(cp * ROWS, ROWS)]
    recv_out[pl.ds(me, 1)] = send_out[pl.ds(slot, 1)]

    def load_rows():
        for w_copy in late:
            w_copy.wait()
        for t in range(3):
            whole = jnp.concatenate(
                [wall[h, base + t * half : base + (t + 1) * half] for h in range(2)], axis=0
            )
            w_fin[t] = whole.astype(F32).T.astype(BF)
        w_bias[...] = jnp.concatenate(
            [wall[h, base + 3 * half : base + 3 * half + 16].astype(F32)[:part] for h in range(2)]
            + [jnp.zeros((8 - heads, n_ch), F32)],
            axis=0,
        ).astype(BF)
        drain(xs.at[pl.ds(0, (ncp - 1) * ROWS)], recv_sem.at[1])

        def load_state(t):
            at = span(t, width)
            row, off = t // (TILES // ROWS), t % (TILES // ROWS)
            tile = xr[row, span(off, width), :].astype(F32).T
            state[:, at] = tile
            gate[:, at] = jax.nn.sigmoid(dot(w_gate[0], norm_columns(tile).astype(BF), (1, 0)))

        steps(TILES, load_state)

    def unpack(load, dst):
        n = n_dev // 8

        def body(t):
            tile = load(t, n).astype(F32).reshape(n * q_rows, lanes)
            dst[span(t, n * q_rows), :] = tile

        steps(8, body)

    def arrived(dst, sem):
        drain(dst.at[pl.ds(0, n_dev - 1)], recv_sem.at[sem])

    def update(t, which):
        at = span(t, width)
        hidden = jnp.concatenate(
            [st_a[pl.ds(t * per + k, n_ch, stride=q_rows), :] for k in range(per)], axis=1
        ).astype(BF)
        step = gate[:, at] * dot(w_fin[which], hidden, (1, 0))
        new = state[:, at] + step
        state[:, at] = new
        delta[:, at] = delta[:, at] + step if which else step
        return new

    def mix_and_return(arm_chunk, back, home, sem, meanwhile):
        n = n_tok // 4
        n_to = n_dev // 4
        y, x, z_of = r // 2, c // np_, lax.rem(c, 2) * np_ + p
        for k in range(4):
            ahead = lax.rem(k + x + z_of, 4)
            m = lax.rem(jnp.where(lax.rem(y, 2) == 0, y + ahead, y + 4 - ahead), 4)
            mixed = dot(arm_chunk(m), arm_b[...], (0, 0))
            for g in range(GROUPS):
                rows = pl.ds(m * (n * GROUPS) + g, n, stride=GROUPS)
                st_c[rows, :] = mixed[:, g * lanes : (g + 1) * lanes]

            def store_back(at, tile):
                back[at] = tile

            pack(st_c, m * n_to, n_to, store_back)

            def body(s, carry, m=m):
                to = m * n_to + lax.rem(me + s * STEP, n_to)
                copy(back.at[to], home.at[slot], sem, to).start()
                return carry

            lax.fori_loop(1, n_to, body, 0)

            @pl.when(m != y)
            def _(body=body):
                body(0, 0)

        home[pl.ds(slot, 1)] = back[pl.ds(me, 1)]
        meanwhile()
        arrived(home, sem)
        m = n_dev // 8

        def sums(t, carry):
            tile = home[pl.ds(t * m, m)].astype(F32)
            return carry[0] + jnp.sum(tile, axis=0), carry[1] + jnp.sum(tile * tile, axis=0)

        zero = jnp.zeros((q_rows, lanes), F32)
        total, squares = zero, zero
        for t in range(8):
            total, squares = sums(t, (total, squares))
        mean = total / n_ch
        scale = lax.rsqrt(squares / n_ch - mean * mean + EPS)

        def normalize(t):
            tile = (home[pl.ds(t * m, m)].astype(F32) - mean[None]) * scale[None]
            st_a[span(t, m * q_rows), :] = tile.reshape(m * q_rows, lanes)

        steps(8, normalize)

    arrived(recv_out, 2)
    left = lax.broadcasted_iota(jnp.int32, (ncp * q_rows, lanes), 1) < block_i

    def lay_out(m, a):
        tiles = [
            recv_out[pl.ds((2 * m + k) * ncp, ncp), a].astype(F32).reshape(ncp * q_rows, lanes)
            for k in range(2)
        ]
        low = jnp.where(left, tiles[0], pltpu.roll(tiles[1], block_i, 1))
        high = jnp.where(left, pltpu.roll(tiles[0], block_i, 1), tiles[1])
        both = [y.reshape(ncp, 1, q_rows, lanes) for y in (low, high)]
        return jnp.concatenate(both, axis=1).reshape(n_tok, lanes).astype(BF)

    for m in range(4):
        arm_b[:, m * lanes : (m + 1) * lanes] = lay_out(m, 1)
    mix_and_return(lambda m: lay_out(m, 0), back_out, home_out, 3, load_rows)

    def in_half(h, first):
        w = wall[pl.ds(h, 1), n_first : 2 * n_first, :].reshape(n_first, n_ch)

        def body(t):
            if first:
                tile = norm_columns(update(t, 0)).astype(BF)
                normed[:, span(t, width)] = tile
            else:
                tile = normed[:, span(t, width)]
            put_arms(w, h, tile, mask_at(mask_r, t), t)

        steps(TILES, body)
        pack_arms(send_in, h * half, half)
        send_half(send_in, recv_in, 4, h)

    in_half(0, True)
    in_half(1, False)
    recv_in[pl.ds(me, 1)] = send_in[pl.ds(slot, 1)]

    def gate_in(t):
        at = span(t, width)
        gate[:, at] = jax.nn.sigmoid(dot(w_gate[1], normed[:, at], (1, 0)))

    steps(TILES, gate_in)
    arrived(recv_in, 4)
    unpack(lambda t, n: recv_in[pl.ds(t * n, n), 0], st_a)
    unpack(lambda t, n: recv_in[pl.ds(t * n, n), 1], st_b)
    for g in range(GROUPS):
        rows = pl.ds(g, n_tok, stride=GROUPS)
        arm_a[:, g * lanes : (g + 1) * lanes] = st_a[rows, :].astype(BF)
        arm_b[:, g * lanes : (g + 1) * lanes] = st_b[rows, :].astype(BF)
    mix_and_return(lambda m: arm_a[:, span(m, lanes)], back_in, home_in, 5, lambda: None)

    def bias_step(t):
        tile = norm_columns(update(t, 1)).astype(BF)
        normed[:, span(t, width)] = tile
        proj = dot(w_bias[...], tile, (1, 0)) * LOG2E
        for k in range(per):
            bias_st[pl.ds(t * per + k, 8, stride=q_rows), :] = proj[:, k * lanes : (k + 1) * lanes]

    steps(TILES, bias_step)
    bias_send[...] = bias_st[: heads * q_rows].astype(BF).reshape(heads, q_rows, lanes)
    def send_head(h):

        def send_bias(s, carry, h=h):
            other = lax.rem(unit + s * STEP, hdev)
            copy(bias_send.at[h], bias_recv.at[h, core, unit], 10 + h, at_unit(other, core)).start()
            return carry

        lax.fori_loop(1, hdev, send_bias, 0)
        bias_recv[h, pl.ds(core, 1), pl.ds(unit, 1)] = bias_send[h][None, None]

    def qkvg(t):
        at = span(t, width)
        tile = normed[:, at]
        row, off = t // (TILES // ROWS), t % (TILES // ROWS)
        keys = []
        m = half
        for h in range(2):
            proj = dot(wall[h, 2 * n_first : 3 * n_first], tile, (1, 0))
            mine = slice(h * m, (h + 1) * m)
            q_t[mine, at] = (proj[:m] * (LOG2E * h_dim**-0.5)).astype(BF)
            keys.append(proj[m : 2 * m])
            v_t[mine, at] = proj[2 * m : 3 * m].astype(BF)
            gate[mine, at] = jax.nn.sigmoid(proj[3 * m :])
        k_n[row, span(off, width), :] = jnp.concatenate(keys, axis=0).T.astype(BF)

    send_head(0)
    send_head(1)
    steps(TILES, qkvg)
    send_head(2)
    send_head(3)
    sibling = (r + 1 - 2 * core) * ncp + cp
    def forward(h):
        drain(bias_recv.at[h, 0, pl.ds(0, hdev - 1)], recv_sem.at[10 + h])
        out = copy(bias_recv.at[h, core], bias_recv.at[h, core], 14 + h, sibling)
        out.start()
        return out

    def finish(i):
        for t in range(TILES // ROWS):
            at = slice(i * n_tok + t * width, i * n_tok + (t + 1) * width)
            gated = (gate[:, at] * att[:, at]).astype(BF)
            total = delta[:, at] + dot(w_fin[2], gated, (1, 0))
            fin_send[i, t * width : (t + 1) * width, :] = total.T.astype(BF)

        def send_final(s, carry):
            to_cp = lax.rem(cp + s, ncp)
            copy(
                fin_send.at[i, pl.ds(to_cp * block_j, block_j), :],
                fin_recv.at[cp * ROWS + i], 7, r * ncp + to_cp,
            ).start()
            return carry

        lax.fori_loop(1, ncp, send_final, 0)

    def attend(h):
        def load(t, n):
            return bias_recv[h, pl.ds(t % 2, 1), pl.ds(t // 2 * n, n)].reshape(n, q_rows, lanes)

        unpack(load, st_a)
        for g in range(GROUPS):
            tile = st_a[pl.ds(g, n_tok, stride=GROUPS), :]
            seen = tm_ref[:, g * lanes : (g + 1) * lanes] > 0
            bias_t[g * lanes : (g + 1) * lanes, :] = jnp.where(seen, tile, -1e30).T
        mine = slice(h * h_dim, (h + 1) * h_dim)

        channel = lax.broadcasted_iota(jnp.int32, (n_ch, n_tok), 0)
        chosen = (channel >= h * h_dim) & (channel < (h + 1) * h_dim)

        def scores_of(i):
            query = q_t[:, i * n_tok : (i + 1) * n_tok].astype(F32)
            return dot(k_n[i], jnp.where(chosen, query, 0.0).astype(BF), (1, 0)) + bias_t[...]

        following = scores_of(0)
        for i in range(ROWS):
            scores = following
            if i + 1 < ROWS:
                following = scores_of(i + 1)
            at = slice(i * n_tok, (i + 1) * n_tok)
            vals = jnp.concatenate([v_t[mine, at], jnp.ones((16, n_tok), BF)], axis=0)
            peak = jnp.max(scores, axis=0, keepdims=True)
            got = dot(vals, jnp.exp2(scores - peak).astype(BF), (1, 0))
            att[mine, at] = got[:h_dim] / got[h_dim : h_dim + 1]
            if h == heads - 1:
                finish(i)

    forwards = [forward(0)]
    for h in range(heads):
        if h + 1 < heads:
            forwards.append(forward(h + 1))
        forwards[h].wait_recv()
        attend(h)

    fin_recv[pl.ds(cp * ROWS, ROWS)] = fin_send[:, pl.ds(cp * block_j, block_j), :]
    drain(fin_recv.at[pl.ds(0, (ncp - 1) * ROWS)], recv_sem.at[7])
    out_ref[...] = fin_recv[...]

    drain(xs.at[pl.ds(0, (ncp - 1) * ROWS)], send_sem.at[1])
    drain(send_out.at[pl.ds(0, n_dev - 1)], send_sem.at[2])
    drain(back_out.at[pl.ds(0, n_dev - 1)], send_sem.at[3])
    drain(send_in.at[pl.ds(0, n_dev - 1)], send_sem.at[4])
    drain(back_in.at[pl.ds(0, n_dev - 1)], send_sem.at[5])
    drain(fin_recv.at[pl.ds(0, (ncp - 1) * ROWS)], send_sem.at[7])
    for h in range(heads):
        drain(bias_recv.at[h, 0, pl.ds(0, hdev - 1)], send_sem.at[10 + h])
        forwards[h].wait_send()


def on_device(
    sizes, pair_input, token_mask,
    out_stack, out_gate, out_final, in_stack, in_gate, in_final, att_stack, att_bias, att_out,
):
    nr, nc, np_ = sizes
    heads = att_bias.shape[1] * np_
    n_dev = nr * nc * np_
    n_ch = n_dev
    n_tok = ROWS * n_dev
    lanes = n_tok // GROUPS
    q_rows = ROWS * GROUPS
    n_pos = ROWS * n_tok
    vm = pltpu.VMEM
    pair_t = (n_ch, n_pos)
    stage = (n_dev * q_rows, lanes)
    two = (n_dev, 2, q_rows, lanes)
    one = (n_dev, q_rows, lanes)
    w_rows = 15 * (n_ch // 2) + 16
    update = pl.pallas_call(
        functools.partial(kernel, (nr, nc, np_, heads)),
        out_shape=jax.ShapeDtypeStruct(pair_input.shape, BF),
        in_specs=[pl.BlockSpec(memory_space=pltpu.VMEM)] * 11,
        out_specs=pl.BlockSpec(memory_space=pltpu.VMEM),
        scratch_shapes=[
            vm((w_rows, n_ch), BF),
            vm((2, w_rows, n_ch), BF),
            vm((2, n_ch, n_ch), BF),
            vm((8, n_ch), BF),
            vm((3, n_ch, n_ch), BF),
            vm((q_rows, lanes), F32),
            vm((q_rows, lanes), F32),
            vm(pair_input.shape, BF),
            vm((ROWS, n_tok, n_ch), BF),
            vm(pair_t, F32),
            vm(pair_t, F32),
            vm(pair_t, F32),
            vm(stage, F32),
            vm(stage, F32),
            vm(stage, F32),
            vm(two, BF), vm(two, BF), vm(one, BF), vm(one, BF),
            vm(two, BF), vm(two, BF), vm(one, BF), vm(one, BF),
            vm((n_tok, n_tok), BF),
            vm((n_tok, n_tok), BF),
            vm(pair_t, BF),
            vm((8 * q_rows, lanes), F32),
            vm((heads, q_rows, lanes), BF),
            vm((heads, 2, n_dev // 2, q_rows, lanes), BF),
            vm((n_tok, n_tok), F32),
            vm(pair_t, BF),
            vm((ROWS, n_tok, n_ch), BF),
            vm(pair_t, BF),
            vm(pair_t, F32),
            vm((ROWS, n_tok, n_ch), BF),
            vm(pair_input.shape, BF),
            pltpu.SemaphoreType.DMA((20,)),
            pltpu.SemaphoreType.DMA((20,)),
        ],
        compiler_params=pltpu.CompilerParams(
            collective_id=0, has_side_effects=True, vmem_limit_bytes=56 * 2**20
        ),
        name="pair_update",
    )(
        pair_input, token_mask[None, :],
        jnp.swapaxes(out_stack, 1, 2), jnp.swapaxes(in_stack, 1, 2), jnp.swapaxes(att_stack, 1, 2),
        out_final, in_final, att_out, att_bias.T, out_gate, in_gate,
    )
    return pair_input + update.astype(F32)


def solution(mesh):
    sizes = tuple(mesh.shape[name] for name in ("row", "col", "chip"))
    return jax.shard_map(
        functools.partial(on_device, sizes),
        mesh=mesh,
        in_specs=(
            P("row", ("col", "chip"), None),
            P(),
            P(None, None, "chip"),
            P(),
            P("chip", None),
            P(None, None, "chip"),
            P(),
            P("chip", None),
            P(None, None, "chip"),
            P(None, "chip"),
            P("chip", None),
        ),
        out_specs=P("row", ("col", "chip"), None),
        check_vma=False,
    )
```
